256 devices in a mesh: east: 8 (over z_hi, core), north: 32 (over y, z_lo, x).
Axes of the slice: x: 4, y: 4, z: 8 (z_hi: 4, z_lo: 2; z = z_hi * 2 + z_lo), core: 2. Of those that a mesh axis runs over, the one named last changes fastest.
Arguments:
- adjoint_start: float32 [5, 128, 1024, 256], P(None, 'east', 'north'), may hold values from -3 to 3
- adjoint_source: float32 [5, 128, 1024, 256], P(None, 'east', 'north'), may hold values from -6 to 6
- base_flow: float32 [3, 128, 1024, 256], P(None, 'east', 'north'), may hold values from -3 to 3
- eddy_visc: float32 [128, 1024, 256], P('east', 'north'), may hold values from 0.1 to 3
- rotor_count: int32 [8, 32], P('east', 'north'), may hold values from 128 to 1024, as said below
- rotor_cell: int32 [8, 32, 1024], P('east', 'north'), may hold values from 0 to 131071
- rotor_turbine: int32 [8, 32, 1024], P('east', 'north'), may hold values from 0 to 383
- rotor_sector: int32 [8, 32, 1024], P('east', 'north'), may hold values from 0 to 7
- rotor_weight: float32 [8, 32, 1024], P('east', 'north'), may hold values from 0.25 to 1
Outputs:
- adjoint_final: float32 [5, 128, 1024, 256], P(None, 'east', 'north')
- thrust_grad: float32 [4, 8, 384], P(None, None, 'north')
The draws below stay inside these ranges and needn't reach their ends.
Inputs may be any that keep to these rules, and one draw needn't show every extreme that they name: `rotor_count`: an eighth of the tiles (at least one), drawn from the seed, hold 1024 live entries; the others hold 128 to 256.
All inputs are finite; a program needn't handle non-finite values.
Results may differ from the reference program's by a relative error of at most 0.0001.
Values sent between devices are 32-bit elements; how exact they have to be, the bound alone decides.
A program may use at most 192 MiB of HBM per device.

```python
import math
import jax
import jax.numpy as jnp

CE = 16
CN = 32
CZ = 256
SLOTS = 1024
SECT = 8
TURB = 384
NE = 128
NN = 1024
N_EAST = 8
N_NORTH = 32


def draw_rotor_count(key, part):
    tiles = N_EAST * N_NORTH
    order = jax.random.permutation(jax.random.fold_in(key, 11), tiles)
    normal_load = jax.random.randint(jax.random.fold_in(key, 12), (tiles,), SLOTS // 8, SLOTS // 4 + 1)
    wake = order < max(1, tiles // 8)
    counts = jnp.where(wake, SLOTS, normal_load).astype(jnp.int32)
    return counts.reshape(N_EAST, N_NORTH)


def set_ends(drawn, stream_key, least, largest):
    extent = drawn.shape
    index_at = [jax.random.randint(jax.random.fold_in(stream_key, axis), (), 0, extent[axis]) for axis in range(len(extent))]
    drawn = drawn.at[tuple(index_at)].set(least)
    longest = extent.index(max(extent))
    index_at[longest] = (index_at[longest] + 1) % extent[longest]
    return drawn.at[tuple(index_at)].set(largest)


def block_levels(rng, dims, cuts, low, high):
    loudness, own = 1.0, jax.random.fold_in(rng, 6)
    for axis_at, blocks in cuts:
        steps = jnp.exp(jax.random.uniform(jax.random.fold_in(own, axis_at), (blocks,), jnp.float32, low / len(cuts), high / len(cuts)))
        loudness = loudness * jnp.repeat(steps, dims[axis_at] // blocks).reshape([-1 if axis == axis_at else 1 for axis in range(len(dims))])
    return loudness


def noise(rng, dims, deviation, limit, pieces=(), held_as=jnp.bfloat16):
    values = deviation * jax.random.normal(rng, dims, jnp.float32)
    if pieces:
        values = values * block_levels(rng, dims, pieces, -0.22, 0.18)
    return jnp.clip(values, -limit, limit).astype(held_as)


def setup_inputs(seed: int = 0) -> dict:
    streams_of = jax.random.split(jax.random.key(seed), 10)
    return {
        "adjoint_start": noise(streams_of[0], (5, NE, NN, CZ), 0.5, 3.0, ((1, 8), (2, 32)), jnp.float32),
        "adjoint_source": noise(streams_of[1], (5, NE, NN, CZ), 1.0, 6.0, ((1, 8), (2, 32)), jnp.float32),
        "base_flow": noise(streams_of[2], (3, NE, NN, CZ), 0.7, 3.0, ((1, 8), (2, 32)), jnp.float32),
        "eddy_visc": jnp.clip(jnp.exp(math.log(3.0) - 3.4011974 * jax.random.uniform(streams_of[3], (NE, NN, CZ), jnp.float32) ** block_levels(streams_of[3], (NE, NN, CZ), ((0, 8), (1, 32)), -0.2, 0.2)), 0.1, 3.0),
        "rotor_count": draw_rotor_count(jax.random.fold_in(streams_of[9], 71), 0),
        "rotor_cell": set_ends(jax.random.randint(streams_of[5], (N_EAST, N_NORTH, SLOTS), 0, CE * CN * CZ), jax.random.fold_in(streams_of[5], 1), 0, (CE * CN * CZ) - 1).astype(jnp.int32),
        "rotor_turbine": set_ends(jax.random.randint(streams_of[6], (N_EAST, N_NORTH, SLOTS), 0, TURB), jax.random.fold_in(streams_of[6], 1), 0, TURB - 1).astype(jnp.int32),
        "rotor_sector": set_ends(jax.random.randint(streams_of[7], (N_EAST, N_NORTH, SLOTS), 0, SECT), jax.random.fold_in(streams_of[7], 1), 0, SECT - 1).astype(jnp.int32),
        "rotor_weight": jnp.clip(0.25 + 0.75 * jax.random.uniform(streams_of[8], (N_EAST, N_NORTH, SLOTS), jnp.float32) ** block_levels(streams_of[8], (N_EAST, N_NORTH, SLOTS), ((0, 8), (1, 32)), -0.2, 0.2), 0.25, 1.0),
    }


def spread(field):
    return jnp.pad(field, ((0, 0), (0, 0), (0, 0), (1, 1)))


def beside_all(padded):
    total = padded[:, 2:, 1:-1, 1:-1] + padded[:, :-2, 1:-1, 1:-1]
    total = total + padded[:, 1:-1, 2:, 1:-1] + padded[:, 1:-1, :-2, 1:-1]
    return total + padded[:, 1:-1, 1:-1, 2:] + padded[:, 1:-1, 1:-1, :-2]


def slopes(padded):
    return [padded[:, 2:, 1:-1, 1:-1] - padded[:, :-2, 1:-1, 1:-1],
            padded[:, 1:-1, 2:, 1:-1] - padded[:, 1:-1, :-2, 1:-1],
            padded[:, 1:-1, 1:-1, 2:] - padded[:, 1:-1, 1:-1, :-2]]


def relax(state_pad, base_pad, source):
    full = spread(state_pad)
    base_full = spread(base_pad)
    centre = full[:, 1:-1, 1:-1, 1:-1]
    base_centre = base_full[:, 1:-1, 1:-1, 1:-1]
    neighbours = beside_all(full)
    diffs = slopes(full)
    velocity_base = base_centre[:3]
    viscous = 1.0 + base_centre[3]
    convect = velocity_base[0] * diffs[0][:3] + velocity_base[1] * diffs[1][:3] + velocity_base[2] * diffs[2][:3]
    pressure_grad = jnp.stack([diffs[0][3], diffs[1][3], diffs[2][3]])
    velocity = (source[:3] + viscous * neighbours[:3] + 0.5 * convect - 0.5 * pressure_grad) / (6.0 * viscous + 1.0)
    diverge = diffs[0][0] + diffs[1][1] + diffs[2][2]
    pressure = (source[3] + neighbours[3] - 0.5 * diverge) / 7.0
    curvature = beside_all(base_full[:3]) - 6.0 * velocity_base
    eddy_new = (source[4] + viscous * neighbours[4] + 0.25 * jnp.sum(centre[:3] * curvature, axis=0)) / (6.0 * viscous + 2.0)
    return jnp.concatenate([velocity, pressure[None], eddy_new[None]], axis=0)


def rim_pad(field):
    return jnp.pad(field, ((0, 0), (1, 1), (1, 1), (0, 0)))


def reference(adjoint_start, adjoint_source, base_flow, eddy_visc, rotor_count, rotor_cell, rotor_turbine, rotor_sector, rotor_weight):
    base_four = jnp.concatenate([base_flow, eddy_visc[None]], axis=0)
    base_pad = rim_pad(base_four)
    state = adjoint_start
    for sweep in range(2):
        state = relax(rim_pad(state), base_pad, adjoint_source)
    east_tile = jnp.arange(N_EAST, dtype=jnp.int32)[:, None, None]
    north_tile = jnp.arange(N_NORTH, dtype=jnp.int32)[None, :, None]
    cell_east = rotor_cell // (CN * CZ) + east_tile * CE
    cell_north = (rotor_cell // CZ) % CN + north_tile * CN
    cell_level = rotor_cell % CZ
    values = state[:, cell_east, cell_north, cell_level]
    chosen = jnp.stack([values[0], values[1], values[2], values[4]])
    upstream = base_flow[0, cell_east, cell_north, cell_level]
    live = jnp.arange(SLOTS, dtype=jnp.int32)[None, None, :] < rotor_count[:, :, None]
    factor = jnp.where(live, rotor_weight * upstream * jnp.abs(upstream), 0.0)
    terms = (chosen * factor[None]).reshape(4, -1)
    segment = (rotor_sector * TURB + rotor_turbine).reshape(-1)
    summed = jax.vmap(lambda row: jax.ops.segment_sum(row, segment, num_segments=SECT * TURB))(terms)
    return state, summed.reshape(4, SECT, TURB)
```

```python
import functools

import jax
import jax.numpy as jnp
from jax import lax
from jax.experimental import pallas as pl
from jax.experimental.pallas import tpu as pltpu
from jax.sharding import PartitionSpec as P

SECT = 8
TURB_DEV = 12
PITCH = 16
PAD = 8
MESH = pl.DeviceIdType.MESH
F32, BF16, I32 = jnp.float32, jnp.bfloat16, jnp.int32

VQ, EDDY, BASE = 0, 1, 2
EAST_UP, EAST_DOWN, NORTH_UP, NORTH_DOWN = 0, 1, 2, 3


def split(x):
    high = x.astype(BF16)
    return high, (x - high.astype(F32)).astype(BF16)


def kernel(
    n_east,
    n_north,
    start,
    source,
    base,
    eddy,
    count,
    cell,
    turbine,
    sector,
    weight,
    final,
    grad,
    v0,
    v1,
    v2,
    flow,
    visc,
    src,
    coef,
    rest,
    curve,
    levels,
    parts,
    gathered,
    totals,
    load_sem,
    out_sem,
    send_sem,
    recv_sem,
    part_send,
    part_recv,
    total_send,
    total_recv,
):
    _, ce, cn, cz = start.shape
    slots = cell.shape[-1]
    east, north = lax.axis_index("east"), lax.axis_index("north")
    rows, planes = pl.ds(PAD, cn), pl.ds(1, ce)

    loads = [
        pltpu.make_async_copy(eddy, visc, load_sem.at[0]),
        pltpu.make_async_copy(base, flow.at[:, planes, rows, :], load_sem.at[1]),
        pltpu.make_async_copy(start.at[0:4], v0.at[0:4, planes, rows, :], load_sem.at[2]),
        pltpu.make_async_copy(source, src, load_sem.at[3]),
        pltpu.make_async_copy(start.at[4:5], v0.at[4:5, planes, rows, :], load_sem.at[4]),
    ]
    for load in loads:
        load.start()

    barrier = pltpu.get_barrier_semaphore()

    def greet_north(k, carry):
        pl.semaphore_signal(barrier, inc=1, device_id={"north": lax.rem(north + k, n_north)}, device_id_type=MESH)
        return carry

    def greet_east(k, carry):
        pl.semaphore_signal(barrier, inc=1, device_id={"east": lax.rem(east + k, n_east)}, device_id_type=MESH)
        return carry

    lax.fori_loop(1, n_north, greet_north, 0)
    lax.fori_loop(1, n_east, greet_east, 0)

    def clear(at_end, plane, row):
        @pl.when(at_end)
        def _():
            for ref in (v0, v1, flow):
                if row is None:
                    ref[:, plane, rows, :] = jnp.zeros((ref.shape[0], cn, cz), F32)
                else:
                    ref[:, planes, row : row + 1, :] = jnp.zeros((ref.shape[0], ce, 1, cz), F32)

    clear(east == 0, 0, None)
    clear(east == n_east - 1, ce + 1, None)
    clear(north == 0, None, PAD - 1)
    clear(north == n_north - 1, None, PAD + cn)

    pl.semaphore_wait(barrier, n_north + n_east - 2)

    def halo(sweep, group, sent, landing, fields, padded):
        first, last = (1, ce) if padded else (0, ce - 1)
        low, high = (PAD, PAD + cn - 1) if padded else (0, cn - 1)
        row_all = rows if padded else slice(None)
        plane_all = planes if padded else slice(None)
        ends = [
            (
                sent.at[fields, last, row_all, :],
                landing.at[fields, 0, rows, :],
                {"east": east + 1},
                east < n_east - 1,
                east > 0,
            ),
            (
                sent.at[fields, first, row_all, :],
                landing.at[fields, ce + 1, rows, :],
                {"east": east - 1},
                east > 0,
                east < n_east - 1,
            ),
            (
                sent.at[fields, plane_all, high : high + 1, :],
                landing.at[fields, planes, PAD - 1 : PAD, :],
                {"north": north + 1},
                north < n_north - 1,
                north > 0,
            ),
            (
                sent.at[fields, plane_all, low : low + 1, :],
                landing.at[fields, planes, PAD + cn : PAD + cn + 1, :],
                {"north": north - 1},
                north > 0,
                north < n_north - 1,
            ),
        ]
        return [
            (
                pltpu.make_async_remote_copy(
                    src_ref=a,
                    dst_ref=b,
                    send_sem=send_sem.at[sweep, group, side],
                    recv_sem=recv_sem.at[sweep, group, side],
                    device_id=target,
                    device_id_type=MESH,
                ),
                sends,
                gets,
            )
            for side, (a, b, target, sends, gets) in enumerate(ends)
        ]

    def begin(copy, sends, gets):
        @pl.when(sends)
        def _():
            copy.start()

    def landed(copy, sends, gets):
        @pl.when(gets)
        def _():
            copy.wait_recv()

    def left(copy, sends, gets):
        @pl.when(sends)
        def _():
            copy.wait_send()

    first_vq = halo(0, VQ, start, v0, slice(0, 4), False)
    first_eddy = halo(0, EDDY, start, v0, slice(4, 5), False)
    first_base = halo(0, BASE, base, flow, slice(0, 3), False)
    second_vq = halo(1, VQ, v1, v1, slice(0, 4), True)
    second_eddy = halo(1, EDDY, v1, v1, slice(4, 5), True)

    for group in (first_vq, first_base, first_eddy):
        for copy in group:
            begin(*copy)

    lane = lax.broadcasted_iota(I32, (cn, cz), 1)
    top, bottom = lane == cz - 1, lane == 0

    for load in loads[:2]:
        load.wait()

    def prepare(e, carry):
        w = 1.0 + visc[e]
        r1 = 1.0 / (6.0 * w + 1.0)
        half = 0.5 * r1
        wr = w * r1
        for k in range(3):
            hu = half * flow[k, e + 1, rows, :]
            above, below = wr + hu, wr - hu
            if k == 2:
                above, below = jnp.where(top, 0.0, above), jnp.where(bottom, 0.0, below)
            coef[2 * k, e] = above
            coef[2 * k + 1, e] = below
        coef[6, e] = half
        r2 = 1.0 / (6.0 * w + 2.0)
        rest[0, e] = r2
        rest[1, e] = w * r2
        return carry

    lax.fori_loop(0, ce, prepare, 0)

    entry_cell = cell[0]
    row_of = lax.shift_right_logical(entry_cell, cz.bit_length() - 1)
    level_of = lax.bitwise_and(entry_cell, cz - 1)
    levels[...] = jnp.where(lax.broadcasted_iota(I32, (cz, slots), 0) == level_of, 1.0, 0.0).astype(BF16)
    step = 4
    block_rows = step * cn
    row_iota = lax.broadcasted_iota(I32, (block_rows, slots), 0)

    def gather(read):
        def block(p, acc):
            high, low = split(read(p * step).reshape(block_rows, cz))
            hot = levels[...]
            found = jnp.dot(high, hot, preferred_element_type=F32) + jnp.dot(low, hot, preferred_element_type=F32)
            kept = jnp.where(row_iota == row_of - p * block_rows, found, 0.0)
            return acc + jnp.sum(kept.reshape(block_rows // 8, 8, slots), axis=0)

        acc = lax.fori_loop(0, ce // step, block, jnp.zeros((8, slots), F32))
        return jnp.sum(acc, axis=0, keepdims=True)

    upstream = gather(lambda p: flow[0, pl.ds(p + 1, step), rows, :])
    live = lax.broadcasted_iota(I32, (1, slots), 1) < count[0, 0]
    factor = jnp.where(live, weight[0] * upstream * jnp.abs(upstream), 0.0)

    def shifted(x):
        return pltpu.roll(x, cz - 1, 1), pltpu.roll(x, 1, 1)

    def relax_vq(e, old, new, offset, where_rows):
        def beside(c):
            x = old[c, e + 1, rows, :]
            return (
                x,
                old[c, e + 2, rows, :],
                old[c, e, rows, :],
                old[c, e + 1, pl.ds(PAD + 1, cn), :],
                old[c, e + 1, pl.ds(PAD - 1, cn), :],
                *shifted(x),
            )

        _, qe, qw, qn, qs, qu, qd = beside(3)
        qu, qd = jnp.where(top, 0.0, qu), jnp.where(bottom, 0.0, qd)
        grads = (qe - qw, qn - qs, qu - qd)
        sum_q = qe + qw + qn + qs + qu + qd
        half = coef[6, e]
        r1 = half + half
        diverge = None
        for c in range(3):
            _, *near = beside(c)
            total = r1 * src[c, e] - half * grads[c]
            for k in range(6):
                total = total + coef[k, e] * near[k]
            new[c, e + offset, where_rows, :] = total
            above, below = near[2 * c], near[2 * c + 1]
            if c == 2:
                above, below = jnp.where(top, 0.0, above), jnp.where(bottom, 0.0, below)
            slope = above - below
            diverge = slope if diverge is None else diverge + slope
        new[3, e + offset, where_rows, :] = (src[3, e] + sum_q - 0.5 * diverge) * (1.0 / 7.0)

    def around(ref, c, e):
        x = ref[c, e + 1, rows, :]
        up, down = shifted(x)
        up, down = jnp.where(top, 0.0, up), jnp.where(bottom, 0.0, down)
        total = ref[c, e + 2, rows, :] + ref[c, e, rows, :]
        total = total + ref[c, e + 1, pl.ds(PAD + 1, cn), :] + ref[c, e + 1, pl.ds(PAD - 1, cn), :]
        return total + up + down, x

    def relax_eddy(e, old, new, offset, where_rows, first):
        sum_m, _ = around(old, 4, e)
        total = rest[0, e] * src[4, e] + rest[1, e] * sum_m
        turn = None
        for c in range(3):
            if first:
                sum_u, u = around(flow, c, e)
                bend = (0.25 * rest[0, e]) * (sum_u - 6.0 * u)
                curve[c, e] = bend
            else:
                bend = curve[c, e]
            total = total + old[c, e + 1, rows, :] * bend
        new[4, e + offset, where_rows, :] = total

    def inner(body):
        def step_body(e, carry):
            body(e)
            return carry

        lax.fori_loop(1, ce - 1, step_body, 0)

    for load in loads[2:]:
        load.wait()
    for copy in first_vq[2:]:
        landed(*copy)
    sweep_one = lambda e: relax_vq(e, v0, v1, 1, rows)
    inner(sweep_one)
    for copy in first_vq[:2]:
        landed(*copy)
    sweep_one(0)
    sweep_one(ce - 1)
    for copy in second_vq:
        begin(*copy)

    for group in (first_base, first_eddy):
        for copy in group:
            landed(*copy)
    eddy_one = lambda e: relax_eddy(e, v0, v1, 1, rows, True)

    def every(body):
        def step_body(e, carry):
            body(e)
            return carry

        lax.fori_loop(0, ce, step_body, 0)

    every(eddy_one)
    for copy in second_eddy:
        begin(*copy)

    for copy in second_vq[2:]:
        landed(*copy)
    sweep_two = lambda e: relax_vq(e, v1, v2, 0, slice(None))
    inner(sweep_two)
    for copy in second_vq[:2]:
        landed(*copy)
    sweep_two(0)
    sweep_two(ce - 1)
    stores = [
        pltpu.make_async_copy(v2.at[0:4], final.at[0:4], out_sem.at[0]),
        pltpu.make_async_copy(v2.at[4:5], final.at[4:5], out_sem.at[1]),
    ]
    stores[0].start()
    for copy in second_eddy:
        landed(*copy)
    every(lambda e: relax_eddy(e, v1, v2, 0, slice(None), False))
    stores[1].start()

    values = [gather(lambda p, c=c: v2[c, pl.ds(p, step), :, :]) * factor for c in (0, 1, 2, 4)]
    terms = jnp.concatenate(values + [jnp.zeros((4, slots), F32)], axis=0)
    turbine_of = turbine[0]
    owner_of = lax.shift_right_logical(turbine_of * 5462, 16)
    place_of = sector[0] * PITCH + turbine_of - owner_of * TURB_DEV
    place_hot = jnp.where(lax.broadcasted_iota(I32, (SECT * PITCH, slots), 0) == place_of, 1.0, 0.0).astype(BF16)
    owner_iota = lax.broadcasted_iota(I32, (n_north, 8, slots), 0)
    spread = jnp.where(owner_iota == owner_of[None], terms[None], 0.0).reshape(n_north * 8, slots)
    high, low = split(spread)
    contract = (((1,), (1,)), ((), ()))
    summed = lax.dot_general(high, place_hot, contract, preferred_element_type=F32)
    summed = summed + lax.dot_general(low, place_hot, contract, preferred_element_type=F32)
    parts[...] = summed.reshape(n_north, 8, SECT * PITCH)

    def part_copy(k):
        to = lax.rem(north + k, n_north)
        return pltpu.make_async_remote_copy(
            src_ref=parts.at[to],
            dst_ref=gathered.at[north],
            send_sem=part_send.at[k],
            recv_sem=part_recv.at[k],
            device_id={"north": to},
            device_id_type=MESH,
        )

    def total_copy(k):
        to = lax.rem(east + k, n_east)
        return pltpu.make_async_remote_copy(
            src_ref=totals.at[east],
            dst_ref=totals.at[east],
            send_sem=total_send.at[k],
            recv_sem=total_recv.at[k],
            device_id={"east": to},
            device_id_type=MESH,
        )

    def each(copy_of, act, size):
        def body(k, carry):
            act(copy_of(k))
            return carry

        lax.fori_loop(1, size, body, 0)

    each(part_copy, lambda c: c.start(), n_north)
    gathered[north] = parts[north]
    each(part_copy, lambda c: c.wait_recv(), n_north)
    totals[east] = jnp.sum(gathered[...], axis=0)
    each(total_copy, lambda c: c.start(), n_east)
    each(total_copy, lambda c: c.wait_recv(), n_east)
    whole = jnp.sum(totals[...], axis=0)
    for s in range(SECT):
        cut = whole[:, s * PITCH : s * PITCH + TURB_DEV]
        for c in range(4):
            grad[c, s : s + 1, :] = cut[c : c + 1]

    each(part_copy, lambda c: c.wait_send(), n_north)
    each(total_copy, lambda c: c.wait_send(), n_east)
    for group in (first_vq, first_base, first_eddy, second_vq, second_eddy):
        for copy in group:
            left(*copy)
    for store in stores:
        store.wait()


def shards(n_east, n_north, *arrays):
    start, source, base, eddy, count, cell = arrays[:6]
    _, ce, cn, cz = start.shape
    slots = cell.shape[-1]
    padded = (ce + 2, cn + 2 * PAD, cz)
    hbm, vmem = pl.BlockSpec(memory_space=pl.ANY), pl.BlockSpec(memory_space=pltpu.VMEM)
    return tuple(
        pl.pallas_call(
            functools.partial(kernel, n_east, n_north),
            out_shape=(
                jax.ShapeDtypeStruct(start.shape, F32),
                jax.ShapeDtypeStruct((4, SECT, TURB_DEV), F32),
            ),
            in_specs=[hbm] * 4 + [pl.BlockSpec(memory_space=pltpu.SMEM)] + [vmem] * 4,
            out_specs=(hbm, vmem),
            scratch_shapes=[
                pltpu.VMEM((5, *padded), F32),
                pltpu.VMEM((5, *padded), F32),
                pltpu.VMEM((5, ce, cn, cz), F32),
                pltpu.VMEM((3, *padded), F32),
                pltpu.VMEM((ce, cn, cz), F32),
                pltpu.VMEM((5, ce, cn, cz), F32),
                pltpu.VMEM((7, ce, cn, cz), F32),
                pltpu.VMEM((2, ce, cn, cz), F32),
                pltpu.VMEM((3, ce, cn, cz), F32),
                pltpu.VMEM((cz, slots), BF16),
                pltpu.VMEM((n_north, 8, SECT * PITCH), F32),
                pltpu.VMEM((n_north, 8, SECT * PITCH), F32),
                pltpu.VMEM((n_east, 8, SECT * PITCH), F32),
                pltpu.SemaphoreType.DMA((5,)),
                pltpu.SemaphoreType.DMA((2,)),
                pltpu.SemaphoreType.DMA((2, 3, 4)),
                pltpu.SemaphoreType.DMA((2, 3, 4)),
                pltpu.SemaphoreType.DMA((n_north,)),
                pltpu.SemaphoreType.DMA((n_north,)),
                pltpu.SemaphoreType.DMA((n_east,)),
                pltpu.SemaphoreType.DMA((n_east,)),
            ],
            compiler_params=pltpu.CompilerParams(
                collective_id=0, has_side_effects=True, vmem_limit_bytes=56 * 1024 * 1024
            ),
        )(*arrays)
    )


def solution(mesh):
    fields, scalars = P(None, "east", "north", None), P("east", "north", None)
    return jax.shard_map(
        functools.partial(shards, mesh.shape["east"], mesh.shape["north"]),
        mesh=mesh,
        in_specs=(fields, fields, fields, scalars, P("east", "north"), scalars, scalars, scalars, scalars),
        out_specs=(fields, P(None, None, "north")),
        check_vma=False,
    )
```

```python
import functools

import jax
import jax.numpy as jnp
from jax import lax
from jax.experimental import pallas as pl
from jax.experimental.pallas import tpu as pltpu
from jax.sharding import PartitionSpec as P

SECT = 8
TURB_DEV = 12
PITCH = 16
PAD = 8
MESH = pl.DeviceIdType.MESH
F32, BF16, I32 = jnp.float32, jnp.bfloat16, jnp.int32

VQ, EDDY, BASE = 0, 1, 2
EAST_UP, EAST_DOWN, NORTH_UP, NORTH_DOWN = 0, 1, 2, 3


def split(x):
    high = x.astype(BF16)
    return high, (x - high.astype(F32)).astype(BF16)


def kernel(
    n_east,
    n_north,
    start,
    source,
    base,
    eddy,
    count,
    cell_in,
    turbine_in,
    sector_in,
    weight_in,
    final,
    grad,
    v0,
    v1,
    flow,
    visc,
    src,
    coef,
    rest,
    curve,
    levels,
    found_acc,
    cell,
    turbine,
    sector,
    weight,
    parts,
    gathered,
    middle,
    totals,
    load_sem,
    send_sem,
    recv_sem,
    part_send,
    part_recv,
    total_send,
    total_recv,
):
    _, ce, cn, cz = start.shape
    slots = cell.shape[-1]
    east, north = lax.axis_index("east"), lax.axis_index("north")
    rows, planes = pl.ds(PAD, cn), pl.ds(1, ce)
    y, low_z, x = north // 8, (north // 4) % 2, north % 4
    n_plane, n_line = n_north // 2, n_east * 2
    in_plane, in_line = y * 4 + x, east * 2 + low_z

    def plane_peer(k):
        to = lax.rem(in_plane + k, n_plane)
        return to, {"north": (to // 4) * 8 + low_z * 4 + to % 4}

    def line_peer(k):
        to = lax.rem(in_line + k, n_line)
        return to, {"east": to // 2, "north": y * 8 + (to % 2) * 4 + x}

    loads = [
        pltpu.make_async_copy(eddy, visc, load_sem.at[0]),
        pltpu.make_async_copy(base, flow.at[:, planes, rows, :], load_sem.at[1]),
        pltpu.make_async_copy(cell_in, cell, load_sem.at[2]),
        pltpu.make_async_copy(weight_in, weight, load_sem.at[3]),
        pltpu.make_async_copy(start.at[0:4], v0.at[0:4, planes, rows, :], load_sem.at[4]),
        pltpu.make_async_copy(source, src, load_sem.at[5]),
        pltpu.make_async_copy(start.at[4:5], v0.at[4:5, planes, rows, :], load_sem.at[6]),
        pltpu.make_async_copy(turbine_in, turbine, load_sem.at[7]),
        pltpu.make_async_copy(sector_in, sector, load_sem.at[8]),
    ]

    barrier = pltpu.get_barrier_semaphore()

    def greet(target):
        pl.semaphore_signal(barrier, inc=1, device_id=target, device_id_type=MESH)

    greet({"north": lax.rem(north + 1, n_north)})
    greet({"north": lax.rem(north + n_north - 1, n_north)})
    for k in sorted(range(1, n_line), key=lambda k: (k % 2, min(k, n_line - k))):
        greet(line_peer(k)[1])
    for k in range(1, n_plane):
        greet(plane_peer(k)[1])
    for load in loads:
        load.start()

    def clear(at_end, plane, row):
        @pl.when(at_end)
        def _():
            for ref in (v0, v1, flow):
                if row is None:
                    ref[:, plane, rows, :] = jnp.zeros((ref.shape[0], cn, cz), F32)
                else:
                    ref[:, planes, row : row + 1, :] = jnp.zeros((ref.shape[0], ce, 1, cz), F32)

    clear(east == 0, 0, None)
    clear(east == n_east - 1, ce + 1, None)
    clear(north == 0, None, PAD - 1)
    clear(north == n_north - 1, None, PAD + cn)

    def halo(sweep, group, sent, landing, fields, padded):
        first, last = (1, ce) if padded else (0, ce - 1)
        low, high = (PAD, PAD + cn - 1) if padded else (0, cn - 1)
        row_all = rows if padded else slice(None)
        plane_all = planes if padded else slice(None)
        ends = [
            (
                sent.at[fields, last, row_all, :],
                landing.at[fields, 0, rows, :],
                {"east": east + 1},
                east < n_east - 1,
                east > 0,
            ),
            (
                sent.at[fields, first, row_all, :],
                landing.at[fields, ce + 1, rows, :],
                {"east": east - 1},
                east > 0,
                east < n_east - 1,
            ),
            (
                sent.at[fields, plane_all, high : high + 1, :],
                landing.at[fields, planes, PAD - 1 : PAD, :],
                {"north": north + 1},
                north < n_north - 1,
                north > 0,
            ),
            (
                sent.at[fields, plane_all, low : low + 1, :],
                landing.at[fields, planes, PAD + cn : PAD + cn + 1, :],
                {"north": north - 1},
                north > 0,
                north < n_north - 1,
            ),
        ]
        return [
            (
                pltpu.make_async_remote_copy(
                    src_ref=a,
                    dst_ref=b,
                    send_sem=send_sem.at[sweep, group, side],
                    recv_sem=recv_sem.at[sweep, group, side],
                    device_id=target,
                    device_id_type=MESH,
                ),
                sends,
                gets,
            )
            for side, (a, b, target, sends, gets) in enumerate(ends)
        ]

    def begin(group):
        for copy, sends, _ in group:
            pl.when(sends)(copy.start)

    def landed(group):
        for copy, _, gets in group:
            pl.when(gets)(copy.wait_recv)

    def left(group):
        for copy, sends, _ in group:
            pl.when(sends)(copy.wait_send)

    first_vq = halo(0, VQ, start, v0, slice(0, 4), False)
    first_eddy = halo(0, EDDY, start, v0, slice(4, 5), False)
    first_base = halo(0, BASE, base, flow, slice(0, 3), False)
    second_vq = halo(1, VQ, v1, v1, slice(0, 4), True)
    second_eddy = halo(1, EDDY, v1, v1, slice(4, 5), True)

    pl.semaphore_wait(barrier, n_plane + n_line)
    begin(first_vq)

    lane = lax.broadcasted_iota(I32, (cn, cz), 1)
    top, bottom = lane == cz - 1, lane == 0

    def loop(begin_at, end_at, body):
        def step_body(e, carry):
            body(e)
            return carry

        lax.fori_loop(begin_at, end_at, step_body, 0)

    for load in loads[:4]:
        load.wait()

    def prepare(e):
        w = 1.0 + visc[e]
        r1 = 1.0 / (6.0 * w + 1.0)
        half = 0.5 * r1
        wr = w * r1
        for k in range(3):
            hu = half * flow[k, e + 1, rows, :]
            above, below = wr + hu, wr - hu
            if k == 2:
                above, below = jnp.where(top, 0.0, above), jnp.where(bottom, 0.0, below)
            coef[2 * k, e] = above
            coef[2 * k + 1, e] = below
        coef[6, e] = half
        r2 = 1.0 / (6.0 * w + 2.0)
        rest[0, e] = r2
        rest[1, e] = w * r2

    loop(0, ce, prepare)
    begin(first_eddy)
    begin(first_base)

    entry_cell = cell[0]
    row_of = lax.shift_right_logical(entry_cell, cz.bit_length() - 1)
    level_of = lax.bitwise_and(entry_cell, cz - 1)
    level_hot = jnp.where(lax.broadcasted_iota(I32, (cz, slots), 0) == level_of, 1.0, 0.0).astype(BF16)
    levels[0:cz] = level_hot
    levels[cz : 2 * cz] = level_hot

    def gather(field, first_row):
        block_rows = field.shape[0]
        both = jnp.concatenate(split(field), axis=1)
        found = jnp.dot(both, levels[...], preferred_element_type=F32)
        here = lax.broadcasted_iota(I32, (block_rows, slots), 0) == row_of - first_row
        return jnp.sum(jnp.where(here, found, 0.0).reshape(block_rows // 8, 8, slots), axis=0)

    step = 4

    def upstream_block(p, acc):
        field = flow[0, pl.ds(p * step + 1, step), rows, :].reshape(step * cn, cz)
        return acc + gather(field, p * step * cn)

    upstream = lax.fori_loop(0, ce // step, upstream_block, jnp.zeros((8, slots), F32))
    upstream = jnp.sum(upstream, axis=0, keepdims=True)
    live = lax.broadcasted_iota(I32, (1, slots), 1) < count[0, 0]
    factor = jnp.where(live, weight[0] * upstream * jnp.abs(upstream), 0.0)

    def shifted(x):
        return pltpu.roll(x, cz - 1, 1), pltpu.roll(x, 1, 1)

    def relax_vq(e, old, new, offset, where_rows):
        def beside(c):
            x = old[c, e + 1, rows, :]
            return (
                x,
                old[c, e + 2, rows, :],
                old[c, e, rows, :],
                old[c, e + 1, pl.ds(PAD + 1, cn), :],
                old[c, e + 1, pl.ds(PAD - 1, cn), :],
                *shifted(x),
            )

        _, qe, qw, qn, qs, qu, qd = beside(3)
        qu, qd = jnp.where(top, 0.0, qu), jnp.where(bottom, 0.0, qd)
        grads = (qe - qw, qn - qs, qu - qd)
        sum_q = qe + qw + qn + qs + qu + qd
        half = coef[6, e]
        r1 = half + half
        diverge = None
        for c in range(3):
            _, *near = beside(c)
            total = r1 * src[c, e] - half * grads[c]
            for k in range(6):
                total = total + coef[k, e] * near[k]
            new[c, e + offset, where_rows, :] = total
            above, below = near[2 * c], near[2 * c + 1]
            if c == 2:
                above, below = jnp.where(top, 0.0, above), jnp.where(bottom, 0.0, below)
            slope = above - below
            diverge = slope if diverge is None else diverge + slope
        new[3, e + offset, where_rows, :] = (src[3, e] + sum_q - 0.5 * diverge) * (1.0 / 7.0)

    def around(ref, c, e):
        x = ref[c, e + 1, rows, :]
        up, down = shifted(x)
        up, down = jnp.where(top, 0.0, up), jnp.where(bottom, 0.0, down)
        total = ref[c, e + 2, rows, :] + ref[c, e, rows, :]
        total = total + ref[c, e + 1, pl.ds(PAD + 1, cn), :] + ref[c, e + 1, pl.ds(PAD - 1, cn), :]
        return total + up + down, x

    def relax_eddy(e, old, new, offset, where_rows, first):
        sum_m, _ = around(old, 4, e)
        total = rest[0, e] * src[4, e] + rest[1, e] * sum_m
        for c in range(3):
            if first:
                sum_u, u = around(flow, c, e)
                bend = (0.25 * rest[0, e]) * (sum_u - 6.0 * u)
                curve[c, e] = bend
            else:
                bend = curve[c, e]
            total = total + old[c, e + 1, rows, :] * bend
        new[4, e + offset, where_rows, :] = total

    for load in loads[4:]:
        load.wait()
    landed(first_vq[2:])
    sweep_one = lambda e: relax_vq(e, v0, v1, 1, rows)
    loop(1, ce - 1, sweep_one)
    landed(first_vq[:2])
    sweep_one(0)
    sweep_one(ce - 1)
    begin(second_vq)

    landed(first_eddy)
    landed(first_base)
    eddy_one = lambda e: relax_eddy(e, v0, v1, 1, rows, True)
    eddy_one(0)
    eddy_one(ce - 1)
    begin(second_eddy[:2])
    loop(1, ce - 1, eddy_one)
    begin(second_eddy[2:])

    landed(second_vq[2:])
    sweep_two = lambda e: relax_vq(e, v1, final, 0, slice(None))
    loop(1, ce - 1, sweep_two)
    half_inside = (ce - 2) // 2

    def gather_inside(c):
        acc = jnp.zeros((8, slots), F32)
        for part in range(2):
            p = 1 + part * half_inside
            field = final[c, p : p + half_inside].reshape(half_inside * cn, cz)
            acc = acc + gather(field, p * cn)
        found_acc[c] = acc

    def gather_edges(c):
        return gather(final[c, 0], 0) + gather(final[c, ce - 1], (ce - 1) * cn)

    loop(0, 3, gather_inside)
    landed(second_vq[:2])
    sweep_two(0)
    sweep_two(ce - 1)
    landed(second_eddy[2:])
    eddy_two = lambda e: relax_eddy(e, v1, final, 0, slice(None), False)
    loop(1, ce - 1, eddy_two)
    gather_inside(4)
    landed(second_eddy[:2])
    eddy_two(0)
    eddy_two(ce - 1)

    values = [jnp.sum(found_acc[c] + gather_edges(c), axis=0, keepdims=True) * factor for c in (0, 1, 2, 4)]
    terms = jnp.concatenate(values + [jnp.zeros((4, slots), F32)], axis=0)
    turbine_of = turbine[0]
    owner_of = lax.shift_right_logical(turbine_of * 5462, 16)
    place_of = sector[0] * PITCH + turbine_of - owner_of * TURB_DEV
    block_of = lax.bitwise_and(owner_of, ~7) + 2 * lax.bitwise_and(owner_of, 3)
    block_of = block_of + lax.bitwise_and(lax.shift_right_logical(owner_of, 2), 1)
    place_hot = jnp.where(lax.broadcasted_iota(I32, (SECT * PITCH, slots), 0) == place_of, 1.0, 0.0).astype(BF16)
    block_iota = lax.broadcasted_iota(I32, (n_north, 8, slots), 0)
    spread = jnp.where(block_iota == block_of[None], terms[None], 0.0).reshape(n_north * 8, slots)
    high, low = split(spread)
    contract = (((1,), (1,)), ((), ()))
    summed = lax.dot_general(high, place_hot, contract, preferred_element_type=F32)
    summed = summed + lax.dot_general(low, place_hot, contract, preferred_element_type=F32)
    parts[...] = summed.reshape(n_plane, 2, 8, SECT * PITCH)

    part_copies, total_copies = [], []
    for k in range(1, n_plane):
        to, target = plane_peer(k)
        part_copies.append(
            pltpu.make_async_remote_copy(
                src_ref=parts.at[to],
                dst_ref=gathered.at[in_plane],
                send_sem=part_send.at[k],
                recv_sem=part_recv.at[k],
                device_id=target,
                device_id_type=MESH,
            )
        )
    for k in range(1, n_line):
        to, target = line_peer(k)
        total_copies.append(
            pltpu.make_async_remote_copy(
                src_ref=middle.at[to % 2],
                dst_ref=totals.at[in_line],
                send_sem=total_send.at[k],
                recv_sem=total_recv.at[k],
                device_id=target,
                device_id_type=MESH,
            )
        )
    for copy in part_copies:
        copy.start()
    gathered[in_plane] = parts[in_plane]
    for copy in part_copies:
        copy.wait_recv()
    middle[...] = jnp.sum(gathered[...], axis=0)
    for copy in total_copies:
        copy.start()
    totals[in_line] = middle[low_z]
    for copy in total_copies:
        copy.wait_recv()
    whole = jnp.sum(totals[...], axis=0)
    for s in range(SECT):
        cut = whole[:, s * PITCH : s * PITCH + TURB_DEV]
        for c in range(4):
            grad[c, s : s + 1, :] = cut[c : c + 1]

    for copy in part_copies + total_copies:
        copy.wait_send()
    for group in (first_vq, first_base, first_eddy, second_vq, second_eddy):
        left(group)


def shards(n_east, n_north, *arrays):
    start, source, base, eddy, count, cell = arrays[:6]
    _, ce, cn, cz = start.shape
    slots = cell.shape[-1]
    padded = (ce + 2, cn + 2 * PAD, cz)
    n_plane, n_line = n_north // 2, n_east * 2
    hbm, vmem = pl.BlockSpec(memory_space=pltpu.HBM), pl.BlockSpec(memory_space=pltpu.VMEM)
    return tuple(
        pl.pallas_call(
            functools.partial(kernel, n_east, n_north),
            out_shape=(pltpu.VMEM(start.shape, F32), pltpu.VMEM((4, SECT, TURB_DEV), F32)),
            in_specs=[hbm] * 4 + [pl.BlockSpec(memory_space=pltpu.SMEM)] + [hbm] * 4,
            out_specs=(vmem, vmem),
            scratch_shapes=[
                pltpu.VMEM((5, *padded), F32),
                pltpu.VMEM((5, *padded), F32),
                pltpu.VMEM((3, *padded), F32),
                pltpu.VMEM((ce, cn, cz), F32),
                pltpu.VMEM((5, ce, cn, cz), F32),
                pltpu.VMEM((7, ce, cn, cz), F32),
                pltpu.VMEM((2, ce, cn, cz), F32),
                pltpu.VMEM((3, ce, cn, cz), F32),
                pltpu.VMEM((2 * cz, slots), BF16),
                pltpu.VMEM((5, 8, slots), F32),
                pltpu.VMEM((1, 1, slots), I32),
                pltpu.VMEM((1, 1, slots), I32),
                pltpu.VMEM((1, 1, slots), I32),
                pltpu.VMEM((1, 1, slots), F32),
                pltpu.VMEM((n_plane, 2, 8, SECT * PITCH), F32),
                pltpu.VMEM((n_plane, 2, 8, SECT * PITCH), F32),
                pltpu.VMEM((2, 8, SECT * PITCH), F32),
                pltpu.VMEM((n_line, 8, SECT * PITCH), F32),
                pltpu.SemaphoreType.DMA((9,)),
                pltpu.SemaphoreType.DMA((2, 3, 4)),
                pltpu.SemaphoreType.DMA((2, 3, 4)),
                pltpu.SemaphoreType.DMA((n_plane,)),
                pltpu.SemaphoreType.DMA((n_plane,)),
                pltpu.SemaphoreType.DMA((n_line,)),
                pltpu.SemaphoreType.DMA((n_line,)),
            ],
            compiler_params=pltpu.CompilerParams(
                collective_id=0, has_side_effects=True, vmem_limit_bytes=40 * 1024 * 1024
            ),
        )(*(pltpu.with_memory_space_constraint(x, pltpu.HBM) if x.dtype == F32 or x.ndim > 2 else x for x in arrays))
    )


def solution(mesh):
    fields, scalars = P(None, "east", "north", None), P("east", "north", None)
    return jax.shard_map(
        functools.partial(shards, mesh.shape["east"], mesh.shape["north"]),
        mesh=mesh,
        in_specs=(fields, fields, fields, scalars, P("east", "north"), scalars, scalars, scalars, scalars),
        out_specs=(fields, P(None, None, "north")),
        check_vma=False,
    )
```

```python
import functools

import jax
import jax.numpy as jnp
from jax import lax
from jax.experimental import pallas as pl
from jax.experimental.pallas import tpu as pltpu
from jax.sharding import PartitionSpec as P

SECT = 8
TURB_DEV = 12
PITCH = 16
PAD = 8
MESH = pl.DeviceIdType.MESH
F32, BF16, I32 = jnp.float32, jnp.bfloat16, jnp.int32

VQ, EDDY, BASE = 0, 1, 2
EAST_UP, EAST_DOWN, NORTH_UP, NORTH_DOWN = 0, 1, 2, 3


def split(x):
    high = x.astype(BF16)
    return high, (x - high.astype(F32)).astype(BF16)


def kernel(
    n_east,
    n_north,
    start,
    source,
    base,
    eddy,
    count,
    cell_in,
    turbine_in,
    sector_in,
    weight_in,
    final,
    grad,
    v0,
    v1,
    flow,
    visc,
    src,
    coef,
    rest,
    curve,
    levels,
    found_acc,
    beside_first,
    beside_second,
    cell,
    turbine,
    sector,
    weight,
    parts,
    gathered,
    middle,
    totals,
    load_sem,
    send_sem,
    recv_sem,
    part_send,
    part_recv,
    total_send,
    total_recv,
):
    _, ce, cn, cz = start.shape
    slots = cell.shape[-1]
    east, north = lax.axis_index("east"), lax.axis_index("north")
    rows, planes = pl.ds(PAD, cn), pl.ds(1, ce)
    y, low_z, x = north // 8, (north // 4) % 2, north % 4
    n_plane, n_line = n_north // 2, n_east * 2
    in_plane, in_line = y * 4 + x, east * 2 + low_z

    def plane_peer(k):
        to = lax.rem(in_plane + k, n_plane)
        return to, {"north": (to // 4) * 8 + low_z * 4 + to % 4}

    def line_peer(k):
        to = lax.rem(in_line + k, n_line)
        return to, {"east": to // 2, "north": y * 8 + (to % 2) * 4 + x}

    loads = [
        pltpu.make_async_copy(eddy, visc, load_sem.at[0]),
        pltpu.make_async_copy(base, flow.at[:, planes, rows, :], load_sem.at[1]),
        pltpu.make_async_copy(cell_in, cell, load_sem.at[2]),
        pltpu.make_async_copy(weight_in, weight, load_sem.at[3]),
        pltpu.make_async_copy(start.at[0:4], v0.at[0:4, planes, rows, :], load_sem.at[4]),
        pltpu.make_async_copy(source, src, load_sem.at[5]),
        pltpu.make_async_copy(start.at[4:5], v0.at[4:5, planes, rows, :], load_sem.at[6]),
        pltpu.make_async_copy(turbine_in, turbine, load_sem.at[7]),
        pltpu.make_async_copy(sector_in, sector, load_sem.at[8]),
    ]

    barrier = pltpu.get_barrier_semaphore()

    def greet(target):
        pl.semaphore_signal(barrier, inc=1, device_id=target, device_id_type=MESH)

    greet({"north": lax.rem(north + 1, n_north)})
    greet({"north": lax.rem(north + n_north - 1, n_north)})
    for k in sorted(range(1, n_line), key=lambda k: (k % 2, min(k, n_line - k))):
        greet(line_peer(k)[1])
    for k in range(1, n_plane):
        greet(plane_peer(k)[1])
    for load in loads:
        load.start()

    for ref in (v0, v1, flow):
        for row in (PAD - 1, PAD + cn):
            ref[:, planes, row : row + 1, :] = jnp.zeros((ref.shape[0], ce, 1, cz), F32)
    for ref in (beside_first, beside_second):
        ref[:, :, 1:15, :] = jnp.zeros((ref.shape[0], ce, 14, cz), F32)

    def clear_plane(at_end, plane):
        @pl.when(at_end)
        def _():
            for ref in (v0, v1, flow):
                ref[:, plane, rows, :] = jnp.zeros((ref.shape[0], cn, cz), F32)

    def clear_row(at_end, row):
        @pl.when(at_end)
        def _():
            for ref in (beside_first, beside_second):
                ref[:, :, row : row + 1, :] = jnp.zeros((ref.shape[0], ce, 1, cz), F32)

    clear_plane(east == 0, 0)
    clear_plane(east == n_east - 1, ce + 1)
    clear_row(north == 0, 0)
    clear_row(north == n_north - 1, 15)

    def halo(sweep, group, sent, landing, fields, padded, row_landing, row_fields):
        first, last = (1, ce) if padded else (0, ce - 1)
        low, high = (PAD, PAD + cn - 1) if padded else (0, cn - 1)
        row_all = rows if padded else slice(None)
        plane_all = planes if padded else slice(None)
        ends = [
            (
                sent.at[fields, last, row_all, :],
                landing.at[fields, 0, rows, :],
                {"east": east + 1},
                east < n_east - 1,
                east > 0,
            ),
            (
                sent.at[fields, first, row_all, :],
                landing.at[fields, ce + 1, rows, :],
                {"east": east - 1},
                east > 0,
                east < n_east - 1,
            ),
            (
                sent.at[fields, plane_all, high : high + 1, :],
                row_landing.at[row_fields, :, 0:1, :],
                {"north": north + 1},
                north < n_north - 1,
                north > 0,
            ),
            (
                sent.at[fields, plane_all, low : low + 1, :],
                row_landing.at[row_fields, :, 15:16, :],
                {"north": north - 1},
                north > 0,
                north < n_north - 1,
            ),
        ]
        return [
            (
                pltpu.make_async_remote_copy(
                    src_ref=a,
                    dst_ref=b,
                    send_sem=send_sem.at[sweep, group, side],
                    recv_sem=recv_sem.at[sweep, group, side],
                    device_id=target,
                    device_id_type=MESH,
                ),
                sends,
                gets,
            )
            for side, (a, b, target, sends, gets) in enumerate(ends)
        ]

    def begin(group):
        for copy, sends, _ in group:
            pl.when(sends)(copy.start)

    def landed(group):
        for copy, _, gets in group:
            pl.when(gets)(copy.wait_recv)

    def left(group):
        for copy, sends, _ in group:
            pl.when(sends)(copy.wait_send)

    first_vq = halo(0, VQ, start, v0, slice(0, 4), False, beside_first, slice(0, 4))
    first_eddy = halo(0, EDDY, start, v0, slice(4, 5), False, beside_first, slice(4, 5))
    first_base = halo(0, BASE, base, flow, slice(0, 3), False, beside_first, slice(5, 8))
    second_vq = halo(1, VQ, v1, v1, slice(0, 4), True, beside_second, slice(0, 4))
    second_eddy = halo(1, EDDY, v1, v1, slice(4, 5), True, beside_second, slice(4, 5))

    pl.semaphore_wait(barrier, n_plane + n_line)
    begin(first_vq)

    lane = lax.broadcasted_iota(I32, (cn, cz), 1)
    top, bottom = lane == cz - 1, lane == 0

    def loop(begin_at, end_at, body):
        def step_body(e, carry):
            body(e)
            return carry

        lax.fori_loop(begin_at, end_at, step_body, 0)

    for load in loads[:4]:
        load.wait()

    def prepare(e):
        w = 1.0 + visc[e]
        r1 = 1.0 / (6.0 * w + 1.0)
        half = 0.5 * r1
        wr = w * r1
        for k in range(3):
            hu = half * flow[k, e + 1, rows, :]
            above, below = wr + hu, wr - hu
            if k == 2:
                above, below = jnp.where(top, 0.0, above), jnp.where(bottom, 0.0, below)
            coef[2 * k, e] = above
            coef[2 * k + 1, e] = below
        coef[6, e] = half
        r2 = 1.0 / (6.0 * w + 2.0)
        rest[0, e] = r2
        rest[1, e] = w * r2

    loop(0, ce, prepare)
    begin(first_eddy)
    begin(first_base)

    entry_cell = cell[0]
    row_of = lax.shift_right_logical(entry_cell, cz.bit_length() - 1)
    level_of = lax.bitwise_and(entry_cell, cz - 1)
    level_hot = jnp.where(lax.broadcasted_iota(I32, (cz, slots), 0) == level_of, 1.0, 0.0).astype(BF16)
    levels[0:cz] = level_hot
    levels[cz : 2 * cz] = level_hot

    def gather(field, row_ids, comps):
        block_rows = field.shape[0] // comps
        both = jnp.concatenate(split(field), axis=1)
        found = jnp.dot(both, levels[...], preferred_element_type=F32)
        here = row_ids == row_of
        sums = []
        for c in range(comps):
            kept = jnp.where(here, found[c * block_rows : (c + 1) * block_rows], 0.0)
            sums.append(jnp.sum(kept.reshape(block_rows // 8, 8, slots), axis=0))
        return sums

    step = 4

    def upstream_block(p, acc):
        field = flow[0, pl.ds(p * step + 1, step), rows, :].reshape(step * cn, cz)
        row_ids = lax.broadcasted_iota(I32, (step * cn, slots), 0) + p * step * cn
        return acc + gather(field, row_ids, 1)[0]

    upstream = lax.fori_loop(0, ce // step, upstream_block, jnp.zeros((8, slots), F32))
    upstream = jnp.sum(upstream, axis=0, keepdims=True)
    live = lax.broadcasted_iota(I32, (1, slots), 1) < count[0, 0]
    factor = jnp.where(live, weight[0] * upstream * jnp.abs(upstream), 0.0)

    def shifted(x):
        return pltpu.roll(x, cz - 1, 1), pltpu.roll(x, 1, 1)

    def relax_vq(e, old, new, offset, where_rows):
        def beside(c):
            x = old[c, e + 1, rows, :]
            return (
                x,
                old[c, e + 2, rows, :],
                old[c, e, rows, :],
                old[c, e + 1, pl.ds(PAD + 1, cn), :],
                old[c, e + 1, pl.ds(PAD - 1, cn), :],
                *shifted(x),
            )

        _, qe, qw, qn, qs, qu, qd = beside(3)
        qu, qd = jnp.where(top, 0.0, qu), jnp.where(bottom, 0.0, qd)
        grads = (qe - qw, qn - qs, qu - qd)
        sum_q = qe + qw + qn + qs + qu + qd
        half = coef[6, e]
        r1 = half + half
        diverge = None
        for c in range(3):
            _, *near = beside(c)
            total = r1 * src[c, e] - half * grads[c]
            for k in range(6):
                total = total + coef[k, e] * near[k]
            new[c, e + offset, where_rows, :] = total
            above, below = near[2 * c], near[2 * c + 1]
            if c == 2:
                above, below = jnp.where(top, 0.0, above), jnp.where(bottom, 0.0, below)
            slope = above - below
            diverge = slope if diverge is None else diverge + slope
        new[3, e + offset, where_rows, :] = (src[3, e] + sum_q - 0.5 * diverge) * (1.0 / 7.0)

    def around(ref, c, e):
        x = ref[c, e + 1, rows, :]
        up, down = shifted(x)
        up, down = jnp.where(top, 0.0, up), jnp.where(bottom, 0.0, down)
        total = ref[c, e + 2, rows, :] + ref[c, e, rows, :]
        total = total + ref[c, e + 1, pl.ds(PAD + 1, cn), :] + ref[c, e + 1, pl.ds(PAD - 1, cn), :]
        return total + up + down, x

    def relax_eddy(e, old, new, offset, where_rows, first):
        sum_m, _ = around(old, 4, e)
        total = rest[0, e] * src[4, e] + rest[1, e] * sum_m
        for c in range(3):
            if first:
                sum_u, u = around(flow, c, e)
                bend = (0.25 * rest[0, e]) * (sum_u - 6.0 * u)
                curve[c, e] = bend
            else:
                bend = curve[c, e]
            total = total + old[c, e + 1, rows, :] * bend
        new[4, e + offset, where_rows, :] = total

    def sides():
        return ((0, 0, 3, 1.0), (cn - 8, 8, 2, -1.0))

    def fix_vq(e, landing, new, offset, pad):
        for row, tile, k, sign in sides():
            near = [landing[c, e, tile : tile + 8, :] for c in range(4)]
            here = slice(row, row + 8)
            for c in range(3):
                add = coef[k, e, here, :] * near[c]
                if c == 1:
                    add = add + (sign * coef[6, e, here, :]) * near[3]
                new[c, e + offset, pad + row : pad + row + 8, :] += add
            new[3, e + offset, pad + row : pad + row + 8, :] += (near[3] + (0.5 * sign) * near[1]) * (1.0 / 7.0)

    def fix_eddy(e, landing, old, new, offset, pad, first):
        for row, tile, _, _ in sides():
            here = slice(row, row + 8)
            add = rest[1, e, here, :] * landing[4, e, tile : tile + 8, :]
            if first:
                quarter = 0.25 * rest[0, e, here, :]
                for c in range(3):
                    bend = quarter * landing[5 + c, e, tile : tile + 8, :]
                    curve[c, e, here, :] += bend
                    add = add + old[c, e + 1, PAD + row : PAD + row + 8, :] * bend
            new[4, e + offset, pad + row : pad + row + 8, :] += add

    for load in loads[4:]:
        load.wait()
    vq_one = lambda e: relax_vq(e, v0, v1, 1, rows)
    eddy_one = lambda e: relax_eddy(e, v0, v1, 1, rows, True)
    loop(1, ce - 1, vq_one)
    loop(1, ce - 1, eddy_one)
    landed(first_vq)
    vq_one(0)
    vq_one(ce - 1)
    loop(0, ce, lambda e: fix_vq(e, beside_first, v1, 1, PAD))
    begin(second_vq)
    landed(first_eddy)
    landed(first_base)
    eddy_one(0)
    eddy_one(ce - 1)
    loop(0, ce, lambda e: fix_eddy(e, beside_first, v0, v1, 1, PAD, True))
    begin(second_eddy)

    vq_two = lambda e: relax_vq(e, v1, final, 0, slice(None))
    eddy_two = lambda e: relax_eddy(e, v1, final, 0, slice(None), False)
    loop(1, ce - 1, vq_two)
    loop(1, ce - 1, eddy_two)
    half_inside = (ce - 2) // 2

    def inner_ids(count_rows, first_row):
        ids = lax.broadcasted_iota(I32, (count_rows, slots), 0)
        in_plane_row = lax.rem(ids, cn)
        return jnp.where((in_plane_row == 0) | (in_plane_row == cn - 1), -1, ids + first_row)

    def gather_inside(c):
        acc = jnp.zeros((8, slots), F32)
        for part in range(2):
            p = 1 + part * half_inside
            field = final[c, p : p + half_inside].reshape(half_inside * cn, cz)
            acc = acc + gather(field, inner_ids(half_inside * cn, p * cn), 1)[0]
        found_acc[c] = acc

    loop(0, 3, gather_inside)
    gather_inside(4)
    landed(second_vq)
    vq_two(0)
    vq_two(ce - 1)
    loop(0, ce, lambda e: fix_vq(e, beside_second, final, 0, 0))
    landed(second_eddy)
    eddy_two(0)
    eddy_two(ce - 1)
    loop(0, ce, lambda e: fix_eddy(e, beside_second, v1, final, 0, 0, False))

    edge_fields = []
    for c in (0, 1, 2, 4):
        for plane in (0, ce - 1):
            edge_fields.append(final[c, plane])
        for row in (0, cn - 1):
            edge_fields.append(final[c, :, row, :])
    plane_iota = lax.broadcasted_iota(I32, (ce, slots), 0) * cn
    edge_ids = jnp.concatenate(
        [inner_ids(cn, 0), inner_ids(cn, (ce - 1) * cn), plane_iota, plane_iota + cn - 1], axis=0
    )
    edge_sums = gather(jnp.concatenate(edge_fields, axis=0), edge_ids, 4)
    values = [
        jnp.sum(found_acc[c] + edge, axis=0, keepdims=True) * factor for c, edge in zip((0, 1, 2, 4), edge_sums)
    ]
    terms = jnp.concatenate(values + [jnp.zeros((4, slots), F32)], axis=0)
    turbine_of = turbine[0]
    owner_of = lax.shift_right_logical(turbine_of * 5462, 16)
    place_of = sector[0] * PITCH + turbine_of - owner_of * TURB_DEV
    block_of = lax.bitwise_and(owner_of, ~7) + 2 * lax.bitwise_and(owner_of, 3)
    block_of = block_of + lax.bitwise_and(lax.shift_right_logical(owner_of, 2), 1)
    place_hot = jnp.where(lax.broadcasted_iota(I32, (SECT * PITCH, slots), 0) == place_of, 1.0, 0.0).astype(BF16)
    block_iota = lax.broadcasted_iota(I32, (n_north, 8, slots), 0)
    spread = jnp.where(block_iota == block_of[None], terms[None], 0.0).reshape(n_north * 8, slots)
    high, low = split(spread)
    contract = (((1,), (1,)), ((), ()))
    summed = lax.dot_general(high, place_hot, contract, preferred_element_type=F32)
    summed = summed + lax.dot_general(low, place_hot, contract, preferred_element_type=F32)
    parts[...] = summed.reshape(n_plane, 2, 8, SECT * PITCH)

    part_copies, total_copies = [], []
    for k in range(1, n_plane):
        to, target = plane_peer(k)
        part_copies.append(
            pltpu.make_async_remote_copy(
                src_ref=parts.at[to],
                dst_ref=gathered.at[in_plane],
                send_sem=part_send.at[k],
                recv_sem=part_recv.at[k],
                device_id=target,
                device_id_type=MESH,
            )
        )
    for k in range(1, n_line):
        to, target = line_peer(k)
        total_copies.append(
            pltpu.make_async_remote_copy(
                src_ref=middle.at[to % 2],
                dst_ref=totals.at[in_line],
                send_sem=total_send.at[k],
                recv_sem=total_recv.at[k],
                device_id=target,
                device_id_type=MESH,
            )
        )
    for copy in part_copies:
        copy.start()
    gathered[in_plane] = parts[in_plane]
    for copy in part_copies:
        copy.wait_recv()
    middle[...] = jnp.sum(gathered[...], axis=0)
    for copy in total_copies:
        copy.start()
    totals[in_line] = middle[low_z]
    for copy in total_copies:
        copy.wait_recv()
    whole = jnp.sum(totals[...], axis=0)
    for s in range(SECT):
        cut = whole[:, s * PITCH : s * PITCH + TURB_DEV]
        for c in range(4):
            grad[c, s : s + 1, :] = cut[c : c + 1]

    for copy in part_copies + total_copies:
        copy.wait_send()
    for group in (first_vq, first_base, first_eddy, second_vq, second_eddy):
        left(group)


def shards(n_east, n_north, *arrays):
    start, source, base, eddy, count, cell = arrays[:6]
    _, ce, cn, cz = start.shape
    slots = cell.shape[-1]
    padded = (ce + 2, cn + 2 * PAD, cz)
    n_plane, n_line = n_north // 2, n_east * 2
    hbm, vmem = pl.BlockSpec(memory_space=pltpu.HBM), pl.BlockSpec(memory_space=pltpu.VMEM)
    return tuple(
        pl.pallas_call(
            functools.partial(kernel, n_east, n_north),
            out_shape=(pltpu.VMEM(start.shape, F32), pltpu.VMEM((4, SECT, TURB_DEV), F32)),
            in_specs=[hbm] * 4 + [pl.BlockSpec(memory_space=pltpu.SMEM)] + [hbm] * 4,
            out_specs=(vmem, vmem),
            scratch_shapes=[
                pltpu.VMEM((5, *padded), F32),
                pltpu.VMEM((5, *padded), F32),
                pltpu.VMEM((3, *padded), F32),
                pltpu.VMEM((ce, cn, cz), F32),
                pltpu.VMEM((5, ce, cn, cz), F32),
                pltpu.VMEM((7, ce, cn, cz), F32),
                pltpu.VMEM((2, ce, cn, cz), F32),
                pltpu.VMEM((3, ce, cn, cz), F32),
                pltpu.VMEM((2 * cz, slots), BF16),
                pltpu.VMEM((5, 8, slots), F32),
                pltpu.VMEM((8, ce, 16, cz), F32),
                pltpu.VMEM((5, ce, 16, cz), F32),
                pltpu.VMEM((1, 1, slots), I32),
                pltpu.VMEM((1, 1, slots), I32),
                pltpu.VMEM((1, 1, slots), I32),
                pltpu.VMEM((1, 1, slots), F32),
                pltpu.VMEM((n_plane, 2, 8, SECT * PITCH), F32),
                pltpu.VMEM((n_plane, 2, 8, SECT * PITCH), F32),
                pltpu.VMEM((2, 8, SECT * PITCH), F32),
                pltpu.VMEM((n_line, 8, SECT * PITCH), F32),
                pltpu.SemaphoreType.DMA((9,)),
                pltpu.SemaphoreType.DMA((2, 3, 4)),
                pltpu.SemaphoreType.DMA((2, 3, 4)),
                pltpu.SemaphoreType.DMA((n_plane,)),
                pltpu.SemaphoreType.DMA((n_plane,)),
                pltpu.SemaphoreType.DMA((n_line,)),
                pltpu.SemaphoreType.DMA((n_line,)),
            ],
            compiler_params=pltpu.CompilerParams(
                collective_id=0, has_side_effects=True, vmem_limit_bytes=40 * 1024 * 1024
            ),
        )(*(pltpu.with_memory_space_constraint(x, pltpu.HBM) if x.dtype == F32 or x.ndim > 2 else x for x in arrays))
    )


def solution(mesh):
    fields, scalars = P(None, "east", "north", None), P("east", "north", None)
    return jax.shard_map(
        functools.partial(shards, mesh.shape["east"], mesh.shape["north"]),
        mesh=mesh,
        in_specs=(fields, fields, fields, scalars, P("east", "north"), scalars, scalars, scalars, scalars),
        out_specs=(fields, P(None, None, "north")),
        check_vma=False,
    )
```

```python
import functools

import jax
import jax.numpy as jnp
from jax import lax
from jax.experimental import pallas as pl
from jax.experimental.pallas import tpu as pltpu
from jax.sharding import PartitionSpec as P

SECT = 8
TURB_DEV = 12
PITCH = 16
PAD = 8
MESH = pl.DeviceIdType.MESH
F32, BF16, I32 = jnp.float32, jnp.bfloat16, jnp.int32

VQ, EDDY, BASE = 0, 1, 2
EAST_UP, EAST_DOWN, NORTH_UP, NORTH_DOWN = 0, 1, 2, 3


def split(x):
    high = x.astype(BF16)
    return high, (x - high.astype(F32)).astype(BF16)


def kernel(
    n_east,
    n_north,
    start,
    source,
    base,
    eddy,
    count,
    cell_in,
    turbine_in,
    sector_in,
    weight_in,
    final,
    grad,
    v0,
    v1,
    flow,
    visc,
    src,
    coef,
    rest,
    curve,
    levels,
    found_acc,
    places,
    blocks,
    beside_first,
    beside_second,
    cell,
    turbine,
    sector,
    weight,
    parts,
    gathered,
    middle,
    totals,
    load_sem,
    send_sem,
    recv_sem,
    part_send,
    part_recv,
    total_send,
    total_recv,
):
    _, ce, cn, cz = start.shape
    slots = cell.shape[-1]
    east, north = lax.axis_index("east"), lax.axis_index("north")
    rows, planes = pl.ds(PAD, cn), pl.ds(1, ce)
    y, low_z, x = north // 8, (north // 4) % 2, north % 4
    n_plane, n_line = n_north // 2, n_east * 2
    in_plane, in_line = y * 4 + x, east * 2 + low_z

    def plane_peer(k):
        to = lax.rem(in_plane + k, n_plane)
        return to, {"north": (to // 4) * 8 + low_z * 4 + to % 4}

    def line_peer(k):
        to = lax.rem(in_line + k, n_line)
        return to, {"east": to // 2, "north": y * 8 + (to % 2) * 4 + x}

    loads = [
        pltpu.make_async_copy(eddy, visc, load_sem.at[0]),
        pltpu.make_async_copy(base, flow.at[:, planes, rows, :], load_sem.at[1]),
        pltpu.make_async_copy(cell_in, cell, load_sem.at[2]),
        pltpu.make_async_copy(weight_in, weight, load_sem.at[3]),
        pltpu.make_async_copy(start.at[0:4], v0.at[0:4, planes, rows, :], load_sem.at[4]),
        pltpu.make_async_copy(source, src, load_sem.at[5]),
        pltpu.make_async_copy(start.at[4:5], v0.at[4:5, planes, rows, :], load_sem.at[6]),
        pltpu.make_async_copy(turbine_in, turbine, load_sem.at[7]),
        pltpu.make_async_copy(sector_in, sector, load_sem.at[8]),
    ]

    barrier = pltpu.get_barrier_semaphore()

    def greet(target):
        pl.semaphore_signal(barrier, inc=1, device_id=target, device_id_type=MESH)

    greet({"north": lax.rem(north + 1, n_north)})
    greet({"north": lax.rem(north + n_north - 1, n_north)})
    for k in sorted(range(1, n_line), key=lambda k: (k % 2, min(k, n_line - k))):
        greet(line_peer(k)[1])
    for k in range(1, n_plane):
        greet(plane_peer(k)[1])
    for load in loads:
        load.start()

    for ref in (v0, v1, flow):
        for row in (PAD - 1, PAD + cn):
            ref[:, planes, row : row + 1, :] = jnp.zeros((ref.shape[0], ce, 1, cz), F32)
    for ref in (beside_first, beside_second):
        ref[:, :, 1:15, :] = jnp.zeros((ref.shape[0], ce, 14, cz), F32)

    def clear_plane(at_end, plane):
        @pl.when(at_end)
        def _():
            for ref in (v0, v1, flow):
                ref[:, plane, rows, :] = jnp.zeros((ref.shape[0], cn, cz), F32)

    def clear_row(at_end, row):
        @pl.when(at_end)
        def _():
            for ref in (beside_first, beside_second):
                ref[:, :, row : row + 1, :] = jnp.zeros((ref.shape[0], ce, 1, cz), F32)

    clear_plane(east == 0, 0)
    clear_plane(east == n_east - 1, ce + 1)
    clear_row(north == 0, 0)
    clear_row(north == n_north - 1, 15)

    def halo(sweep, group, sent, landing, fields, padded, row_landing, row_fields):
        first, last = (1, ce) if padded else (0, ce - 1)
        low, high = (PAD, PAD + cn - 1) if padded else (0, cn - 1)
        row_all = rows if padded else slice(None)
        plane_all = planes if padded else slice(None)
        ends = [
            (
                sent.at[fields, last, row_all, :],
                landing.at[fields, 0, rows, :],
                {"east": east + 1},
                east < n_east - 1,
                east > 0,
            ),
            (
                sent.at[fields, first, row_all, :],
                landing.at[fields, ce + 1, rows, :],
                {"east": east - 1},
                east > 0,
                east < n_east - 1,
            ),
            (
                sent.at[fields, plane_all, high : high + 1, :],
                row_landing.at[row_fields, :, 0:1, :],
                {"north": north + 1},
                north < n_north - 1,
                north > 0,
            ),
            (
                sent.at[fields, plane_all, low : low + 1, :],
                row_landing.at[row_fields, :, 15:16, :],
                {"north": north - 1},
                north > 0,
                north < n_north - 1,
            ),
        ]
        return [
            (
                pltpu.make_async_remote_copy(
                    src_ref=a,
                    dst_ref=b,
                    send_sem=send_sem.at[sweep, group, side],
                    recv_sem=recv_sem.at[sweep, group, side],
                    device_id=target,
                    device_id_type=MESH,
                ),
                sends,
                gets,
            )
            for side, (a, b, target, sends, gets) in enumerate(ends)
        ]

    def begin(group):
        for copy, sends, _ in group:
            pl.when(sends)(copy.start)

    def landed(group):
        for copy, _, gets in group:
            pl.when(gets)(copy.wait_recv)

    def left(group):
        for copy, sends, _ in group:
            pl.when(sends)(copy.wait_send)

    first_vq = halo(0, VQ, start, v0, slice(0, 4), False, beside_first, slice(0, 4))
    first_eddy = halo(0, EDDY, start, v0, slice(4, 5), False, beside_first, slice(4, 5))
    first_base = halo(0, BASE, base, flow, slice(0, 3), False, beside_first, slice(5, 8))
    second_vq = halo(1, VQ, v1, v1, slice(0, 4), True, beside_second, slice(0, 4))
    second_eddy = halo(1, EDDY, v1, v1, slice(4, 5), True, beside_second, slice(4, 5))

    pl.semaphore_wait(barrier, n_plane + n_line)
    begin(first_vq)

    lane = lax.broadcasted_iota(I32, (cn, cz), 1)
    top, bottom = lane == cz - 1, lane == 0

    def loop(begin_at, end_at, body):
        def step_body(e, carry):
            body(e)
            return carry

        lax.fori_loop(begin_at, end_at, step_body, 0)

    for load in loads[:4]:
        load.wait()

    def prepare(e):
        w = 1.0 + visc[e]
        r1 = 1.0 / (6.0 * w + 1.0)
        half = 0.5 * r1
        wr = w * r1
        for k in range(3):
            hu = half * flow[k, e + 1, rows, :]
            above, below = wr + hu, wr - hu
            if k == 2:
                above, below = jnp.where(top, 0.0, above), jnp.where(bottom, 0.0, below)
            coef[2 * k, e] = above
            coef[2 * k + 1, e] = below
        coef[6, e] = half
        r2 = 1.0 / (6.0 * w + 2.0)
        rest[0, e] = r2
        rest[1, e] = w * r2

    loop(0, ce, prepare)
    begin(first_eddy)
    begin(first_base)

    entry_cell = cell[0]
    row_of = lax.shift_right_logical(entry_cell, cz.bit_length() - 1)
    level_of = lax.bitwise_and(entry_cell, cz - 1)
    level_hot = jnp.where(lax.broadcasted_iota(I32, (cz, slots), 0) == level_of, 1.0, 0.0).astype(BF16)
    levels[0:cz] = level_hot
    levels[cz : 2 * cz] = level_hot

    def gather(field, row_ids, comps):
        block_rows = field.shape[0] // comps
        both = jnp.concatenate(split(field), axis=1)
        found = jnp.dot(both, levels[...], preferred_element_type=F32)
        here = row_ids == row_of
        sums = []
        for c in range(comps):
            kept = jnp.where(here, found[c * block_rows : (c + 1) * block_rows], 0.0)
            sums.append(jnp.sum(kept.reshape(block_rows // 8, 8, slots), axis=0))
        return sums

    step = 4

    def upstream_block(p, acc):
        field = flow[0, pl.ds(p * step + 1, step), rows, :].reshape(step * cn, cz)
        row_ids = lax.broadcasted_iota(I32, (step * cn, slots), 0) + p * step * cn
        return acc + gather(field, row_ids, 1)[0]

    upstream = lax.fori_loop(0, ce // step, upstream_block, jnp.zeros((8, slots), F32))
    upstream = jnp.sum(upstream, axis=0, keepdims=True)
    live = lax.broadcasted_iota(I32, (1, slots), 1) < count[0, 0]
    factor = jnp.where(live, weight[0] * upstream * jnp.abs(upstream), 0.0)

    for load in loads[7:]:
        load.wait()
    turbine_of = turbine[0]
    owner_of = lax.shift_right_logical(turbine_of * 5462, 16)
    place_of = sector[0] * PITCH + turbine_of - owner_of * TURB_DEV
    block_of = lax.bitwise_and(owner_of, ~7) + 2 * lax.bitwise_and(owner_of, 3)
    block_of = block_of + lax.bitwise_and(lax.shift_right_logical(owner_of, 2), 1)
    places[...] = jnp.where(lax.broadcasted_iota(I32, places.shape, 0) == place_of, 1.0, 0.0).astype(BF16)
    block_iota = lax.shift_right_logical(lax.broadcasted_iota(I32, blocks.shape, 0), 4)
    blocks[...] = jnp.where(block_iota == block_of, 1.0, 0.0).astype(BF16)

    def shifted(x):
        return pltpu.roll(x, cz - 1, 1), pltpu.roll(x, 1, 1)

    def relax_vq(e, old, new, offset, where_rows):
        def beside(c):
            x = old[c, e + 1, rows, :]
            return (
                x,
                old[c, e + 2, rows, :],
                old[c, e, rows, :],
                old[c, e + 1, pl.ds(PAD + 1, cn), :],
                old[c, e + 1, pl.ds(PAD - 1, cn), :],
                *shifted(x),
            )

        _, qe, qw, qn, qs, qu, qd = beside(3)
        qu, qd = jnp.where(top, 0.0, qu), jnp.where(bottom, 0.0, qd)
        grads = (qe - qw, qn - qs, qu - qd)
        sum_q = qe + qw + qn + qs + qu + qd
        half = coef[6, e]
        r1 = half + half
        diverge = None
        for c in range(3):
            _, *near = beside(c)
            total = r1 * src[c, e] - half * grads[c]
            for k in range(6):
                total = total + coef[k, e] * near[k]
            new[c, e + offset, where_rows, :] = total
            above, below = near[2 * c], near[2 * c + 1]
            if c == 2:
                above, below = jnp.where(top, 0.0, above), jnp.where(bottom, 0.0, below)
            slope = above - below
            diverge = slope if diverge is None else diverge + slope
        new[3, e + offset, where_rows, :] = (src[3, e] + sum_q - 0.5 * diverge) * (1.0 / 7.0)

    def around(ref, c, e):
        x = ref[c, e + 1, rows, :]
        up, down = shifted(x)
        up, down = jnp.where(top, 0.0, up), jnp.where(bottom, 0.0, down)
        total = ref[c, e + 2, rows, :] + ref[c, e, rows, :]
        total = total + ref[c, e + 1, pl.ds(PAD + 1, cn), :] + ref[c, e + 1, pl.ds(PAD - 1, cn), :]
        return total + up + down, x

    def relax_eddy(e, old, new, offset, where_rows, first):
        sum_m, _ = around(old, 4, e)
        total = rest[0, e] * src[4, e] + rest[1, e] * sum_m
        for c in range(3):
            if first:
                sum_u, u = around(flow, c, e)
                bend = (0.25 * rest[0, e]) * (sum_u - 6.0 * u)
                curve[c, e] = bend
            else:
                bend = curve[c, e]
            total = total + old[c, e + 1, rows, :] * bend
        new[4, e + offset, where_rows, :] = total

    def sides():
        return ((0, 0, 3, 1.0), (cn - 8, 8, 2, -1.0))

    def fix_vq(e, landing, new, offset, pad):
        for row, tile, k, sign in sides():
            near = [landing[c, e, tile : tile + 8, :] for c in range(4)]
            here = slice(row, row + 8)
            for c in range(3):
                add = coef[k, e, here, :] * near[c]
                if c == 1:
                    add = add + (sign * coef[6, e, here, :]) * near[3]
                new[c, e + offset, pad + row : pad + row + 8, :] += add
            new[3, e + offset, pad + row : pad + row + 8, :] += (near[3] + (0.5 * sign) * near[1]) * (1.0 / 7.0)

    def fix_eddy(e, landing, old, new, offset, pad, first):
        for row, tile, _, _ in sides():
            here = slice(row, row + 8)
            add = rest[1, e, here, :] * landing[4, e, tile : tile + 8, :]
            if first:
                quarter = 0.25 * rest[0, e, here, :]
                for c in range(3):
                    bend = quarter * landing[5 + c, e, tile : tile + 8, :]
                    curve[c, e, here, :] += bend
                    add = add + old[c, e + 1, PAD + row : PAD + row + 8, :] * bend
            new[4, e + offset, pad + row : pad + row + 8, :] += add

    for load in loads[4:7]:
        load.wait()
    vq_one = lambda e: relax_vq(e, v0, v1, 1, rows)
    eddy_one = lambda e: relax_eddy(e, v0, v1, 1, rows, True)
    loop(1, ce - 1, vq_one)
    loop(1, ce - 1, eddy_one)
    landed(first_vq)
    vq_one(0)
    vq_one(ce - 1)
    loop(0, ce, lambda e: fix_vq(e, beside_first, v1, 1, PAD))
    begin(second_vq)
    vq_two = lambda e: relax_vq(e, v1, final, 0, slice(None))
    loop(1, ce - 1, vq_two)
    landed(first_eddy)
    landed(first_base)
    fix_eddy_one = lambda e: fix_eddy(e, beside_first, v0, v1, 1, PAD, True)
    for e in (0, ce - 1):
        eddy_one(e)
        fix_eddy_one(e)
    begin(second_eddy[:2])
    loop(1, ce - 1, fix_eddy_one)
    begin(second_eddy[2:])

    eddy_two = lambda e: relax_eddy(e, v1, final, 0, slice(None), False)
    loop(1, ce - 1, eddy_two)
    half_inside = (ce - 2) // 2

    def inner_ids(count_rows, first_row):
        ids = lax.broadcasted_iota(I32, (count_rows, slots), 0)
        in_plane_row = lax.rem(ids, cn)
        return jnp.where((in_plane_row == 0) | (in_plane_row == cn - 1), -1, ids + first_row)

    def gather_inside(c):
        acc = jnp.zeros((8, slots), F32)
        for part in range(2):
            p = 1 + part * half_inside
            field = final[c, p : p + half_inside].reshape(half_inside * cn, cz)
            acc = acc + gather(field, inner_ids(half_inside * cn, p * cn), 1)[0]
        found_acc[c] = acc

    loop(0, 3, gather_inside)
    gather_inside(4)
    landed(second_vq)
    vq_two(0)
    vq_two(ce - 1)
    loop(0, ce, lambda e: fix_vq(e, beside_second, final, 0, 0))
    landed(second_eddy)
    eddy_two(0)
    eddy_two(ce - 1)
    loop(0, ce, lambda e: fix_eddy(e, beside_second, v1, final, 0, 0, False))

    edge_fields = []
    for c in (0, 1, 2, 4):
        for plane in (0, ce - 1):
            edge_fields.append(final[c, plane])
        for row in (0, cn - 1):
            edge_fields.append(final[c, :, row, :])
    plane_iota = lax.broadcasted_iota(I32, (ce, slots), 0) * cn
    edge_ids = jnp.concatenate(
        [inner_ids(cn, 0), inner_ids(cn, (ce - 1) * cn), plane_iota, plane_iota + cn - 1], axis=0
    )
    edge_sums = gather(jnp.concatenate(edge_fields, axis=0), edge_ids, 4)
    values = [
        jnp.sum(found_acc[c] + edge, axis=0, keepdims=True) * factor for c, edge in zip((0, 1, 2, 4), edge_sums)
    ]
    terms = jnp.concatenate(values + [jnp.zeros((4, slots), F32)], axis=0)
    both = jnp.concatenate(split(terms), axis=0)
    spread = blocks[...] * jnp.concatenate([both] * n_north, axis=0)
    contract = (((1,), (1,)), ((), ()))
    summed = lax.dot_general(spread, places[...], contract, preferred_element_type=F32)
    summed = jnp.sum(summed.reshape(n_north, 2, 8, SECT * PITCH), axis=1)
    parts[...] = summed.reshape(n_plane, 2, 8, SECT * PITCH)

    part_copies, total_copies = [], []
    for k in range(1, n_plane):
        to, target = plane_peer(k)
        part_copies.append(
            pltpu.make_async_remote_copy(
                src_ref=parts.at[to],
                dst_ref=gathered.at[in_plane],
                send_sem=part_send.at[k],
                recv_sem=part_recv.at[k],
                device_id=target,
                device_id_type=MESH,
            )
        )
    for k in range(1, n_line):
        to, target = line_peer(k)
        total_copies.append(
            pltpu.make_async_remote_copy(
                src_ref=middle.at[to % 2],
                dst_ref=totals.at[in_line],
                send_sem=total_send.at[k],
                recv_sem=total_recv.at[k],
                device_id=target,
                device_id_type=MESH,
            )
        )
    for copy in part_copies:
        copy.start()
    gathered[in_plane] = parts[in_plane]
    for copy in part_copies:
        copy.wait_recv()
    middle[...] = jnp.sum(gathered[...], axis=0)
    for copy in total_copies:
        copy.start()
    totals[in_line] = middle[low_z]
    for copy in total_copies:
        copy.wait_recv()
    whole = jnp.sum(totals[...], axis=0)
    for s in range(SECT):
        cut = whole[:, s * PITCH : s * PITCH + TURB_DEV]
        for c in range(4):
            grad[c, s : s + 1, :] = cut[c : c + 1]

    for copy in part_copies + total_copies:
        copy.wait_send()
    for group in (first_vq, first_base, first_eddy, second_vq, second_eddy):
        left(group)


def store(fields, sums, fields_out, sums_out, sem):
    copies = [pltpu.make_async_copy(sums, sums_out, sem.at[0])]
    copies += [pltpu.make_async_copy(fields.at[c], fields_out.at[c], sem.at[c + 1]) for c in range(fields.shape[0])]
    for copy in copies:
        copy.start()
    for copy in copies:
        copy.wait()


def shards(n_east, n_north, *arrays):
    start, source, base, eddy, count, cell = arrays[:6]
    _, ce, cn, cz = start.shape
    slots = cell.shape[-1]
    padded = (ce + 2, cn + 2 * PAD, cz)
    n_plane, n_line = n_north // 2, n_east * 2
    hbm, vmem = pl.BlockSpec(memory_space=pltpu.HBM), pl.BlockSpec(memory_space=pltpu.VMEM)
    in_vmem = (
        pl.pallas_call(
            functools.partial(kernel, n_east, n_north),
            out_shape=(pltpu.VMEM(start.shape, F32), pltpu.VMEM((4, SECT, TURB_DEV), F32)),
            in_specs=[hbm] * 4 + [pl.BlockSpec(memory_space=pltpu.SMEM)] + [hbm] * 4,
            out_specs=(vmem, vmem),
            scratch_shapes=[
                pltpu.VMEM((5, *padded), F32),
                pltpu.VMEM((5, *padded), F32),
                pltpu.VMEM((3, *padded), F32),
                pltpu.VMEM((ce, cn, cz), F32),
                pltpu.VMEM((5, ce, cn, cz), F32),
                pltpu.VMEM((7, ce, cn, cz), F32),
                pltpu.VMEM((2, ce, cn, cz), F32),
                pltpu.VMEM((3, ce, cn, cz), F32),
                pltpu.VMEM((2 * cz, slots), BF16),
                pltpu.VMEM((5, 8, slots), F32),
                pltpu.VMEM((SECT * PITCH, slots), BF16),
                pltpu.VMEM((n_north * 16, slots), BF16),
                pltpu.VMEM((8, ce, 16, cz), F32),
                pltpu.VMEM((5, ce, 16, cz), F32),
                pltpu.VMEM((1, 1, slots), I32),
                pltpu.VMEM((1, 1, slots), I32),
                pltpu.VMEM((1, 1, slots), I32),
                pltpu.VMEM((1, 1, slots), F32),
                pltpu.VMEM((n_plane, 2, 8, SECT * PITCH), F32),
                pltpu.VMEM((n_plane, 2, 8, SECT * PITCH), F32),
                pltpu.VMEM((2, 8, SECT * PITCH), F32),
                pltpu.VMEM((n_line, 8, SECT * PITCH), F32),
                pltpu.SemaphoreType.DMA((9,)),
                pltpu.SemaphoreType.DMA((2, 3, 4)),
                pltpu.SemaphoreType.DMA((2, 3, 4)),
                pltpu.SemaphoreType.DMA((n_plane,)),
                pltpu.SemaphoreType.DMA((n_plane,)),
                pltpu.SemaphoreType.DMA((n_line,)),
                pltpu.SemaphoreType.DMA((n_line,)),
            ],
            compiler_params=pltpu.CompilerParams(
                collective_id=0, has_side_effects=True, vmem_limit_bytes=40 * 1024 * 1024
            ),
        )(*(pltpu.with_memory_space_constraint(x, pltpu.HBM) if x.dtype == F32 or x.ndim > 2 else x for x in arrays))
    )
    parts = start.shape[0]
    return tuple(
        pl.pallas_call(
            store,
            out_shape=tuple(jax.ShapeDtypeStruct(x.shape, x.dtype) for x in in_vmem),
            in_specs=[vmem] * 2,
            out_specs=(hbm, hbm),
            scratch_shapes=[pltpu.SemaphoreType.DMA((parts + 1,))],
            compiler_params=pltpu.CompilerParams(vmem_limit_bytes=8 * 1024 * 1024),
        )(*(pltpu.with_memory_space_constraint(x, pltpu.VMEM) for x in in_vmem))
    )


def solution(mesh):
    fields, scalars = P(None, "east", "north", None), P("east", "north", None)
    return jax.shard_map(
        functools.partial(shards, mesh.shape["east"], mesh.shape["north"]),
        mesh=mesh,
        in_specs=(fields, fields, fields, scalars, P("east", "north"), scalars, scalars, scalars, scalars),
        out_specs=(fields, P(None, None, "north")),
        check_vma=False,
    )
```

```python
import functools

import jax
import jax.numpy as jnp
from jax import lax
from jax.experimental import pallas as pl
from jax.experimental.pallas import tpu as pltpu
from jax.sharding import PartitionSpec as P

SECT = 8
TURB_DEV = 12
PITCH = 16
PAD = 8
MESH = pl.DeviceIdType.MESH
F32, BF16, I32 = jnp.float32, jnp.bfloat16, jnp.int32

VQ, EDDY, BASE = 0, 1, 2
EAST_UP, EAST_DOWN, NORTH_UP, NORTH_DOWN = 0, 1, 2, 3


def split(x):
    high = x.astype(BF16)
    return high, (x - high.astype(F32)).astype(BF16)


def kernel(
    n_east,
    n_north,
    start,
    source,
    base,
    eddy,
    count,
    cell_in,
    turbine_in,
    sector_in,
    weight_in,
    final,
    grad,
    v0,
    v1,
    flow,
    visc,
    src,
    coef,
    rest,
    curve,
    levels,
    found_acc,
    places,
    blocks,
    beside_first,
    beside_second,
    cell,
    turbine,
    sector,
    weight,
    parts,
    gathered,
    middle,
    totals,
    load_sem,
    send_sem,
    recv_sem,
    part_send,
    part_recv,
    total_send,
    total_recv,
):
    _, ce, cn, cz = start.shape
    slots = cell.shape[-1]
    east, north = lax.axis_index("east"), lax.axis_index("north")
    rows, planes = pl.ds(PAD, cn), pl.ds(1, ce)
    y, low_z, x = north // 8, (north // 4) % 2, north % 4
    n_plane, n_line = n_north // 2, n_east * 2
    in_plane, in_line = y * 4 + x, east * 2 + low_z

    n_y, n_z = n_plane // 4, n_east
    z = east // 2 * 2 + low_z
    core = east % 2

    def hops(step, size):
        return min(step, size - step)

    plane_steps = [(dy, dx) for dy in range(n_y) for dx in range(4) if (dy, dx) != (0, 0)]
    plane_steps.sort(key=lambda d: -hops(d[0], n_y) - hops(d[1], 4))
    line_steps = [(dz, flip) for dz in range(n_z) for flip in range(2) if (dz, flip) != (0, 0)]
    line_steps.sort(key=lambda d: -2 * hops(d[0], n_z) - d[1])

    def plane_peer(k):
        dy, dx = plane_steps[k - 1]
        to_y, to_x = lax.rem(y + dy, n_y), lax.rem(x + dx, 4)
        return to_y * 4 + to_x, {"north": to_y * 8 + low_z * 4 + to_x}

    def line_peer(k):
        dz, flip = line_steps[k - 1]
        to_z = lax.rem(z + dz, n_z)
        to_core = 1 - core if flip else core
        to_east, to_low = to_z // 2 * 2 + to_core, to_z % 2
        return to_east * 2 + to_low, {"east": to_east, "north": y * 8 + to_low * 4 + x}

    loads = [
        pltpu.make_async_copy(eddy, visc, load_sem.at[0]),
        pltpu.make_async_copy(base, flow.at[:, planes, rows, :], load_sem.at[1]),
        pltpu.make_async_copy(cell_in, cell, load_sem.at[2]),
        pltpu.make_async_copy(weight_in, weight, load_sem.at[3]),
        pltpu.make_async_copy(start.at[0:4], v0.at[0:4, planes, rows, :], load_sem.at[4]),
        pltpu.make_async_copy(source, src, load_sem.at[5]),
        pltpu.make_async_copy(start.at[4:5], v0.at[4:5, planes, rows, :], load_sem.at[6]),
        pltpu.make_async_copy(turbine_in, turbine, load_sem.at[7]),
        pltpu.make_async_copy(sector_in, sector, load_sem.at[8]),
    ]

    barrier = pltpu.get_barrier_semaphore()

    def greet(target):
        pl.semaphore_signal(barrier, inc=1, device_id=target, device_id_type=MESH)

    greet({"north": lax.rem(north + 1, n_north)})
    greet({"north": lax.rem(north + n_north - 1, n_north)})
    for k in range(n_line - 1, 0, -1):
        greet(line_peer(k)[1])
    for k in range(1, n_plane):
        greet(plane_peer(k)[1])
    for load in loads:
        load.start()

    for ref in (v0, v1, flow):
        for row in (PAD - 1, PAD + cn):
            ref[:, planes, row : row + 1, :] = jnp.zeros((ref.shape[0], ce, 1, cz), F32)
    for ref in (beside_first, beside_second):
        ref[:, :, 1:15, :] = jnp.zeros((ref.shape[0], ce, 14, cz), F32)

    def clear_plane(at_end, plane):
        @pl.when(at_end)
        def _():
            for ref in (v0, v1, flow):
                ref[:, plane, rows, :] = jnp.zeros((ref.shape[0], cn, cz), F32)

    def clear_row(at_end, row):
        @pl.when(at_end)
        def _():
            for ref in (beside_first, beside_second):
                ref[:, :, row : row + 1, :] = jnp.zeros((ref.shape[0], ce, 1, cz), F32)

    clear_plane(east == 0, 0)
    clear_plane(east == n_east - 1, ce + 1)
    clear_row(north == 0, 0)
    clear_row(north == n_north - 1, 15)

    def halo(sweep, group, sent, landing, fields, padded, row_landing, row_fields):
        first, last = (1, ce) if padded else (0, ce - 1)
        low, high = (PAD, PAD + cn - 1) if padded else (0, cn - 1)
        row_all = rows if padded else slice(None)
        plane_all = planes if padded else slice(None)
        ends = [
            (
                sent.at[fields, last, row_all, :],
                landing.at[fields, 0, rows, :],
                {"east": east + 1},
                east < n_east - 1,
                east > 0,
            ),
            (
                sent.at[fields, first, row_all, :],
                landing.at[fields, ce + 1, rows, :],
                {"east": east - 1},
                east > 0,
                east < n_east - 1,
            ),
            (
                sent.at[fields, plane_all, high : high + 1, :],
                row_landing.at[row_fields, :, 0:1, :],
                {"north": north + 1},
                north < n_north - 1,
                north > 0,
            ),
            (
                sent.at[fields, plane_all, low : low + 1, :],
                row_landing.at[row_fields, :, 15:16, :],
                {"north": north - 1},
                north > 0,
                north < n_north - 1,
            ),
        ]
        return [
            (
                pltpu.make_async_remote_copy(
                    src_ref=a,
                    dst_ref=b,
                    send_sem=send_sem.at[sweep, group, side],
                    recv_sem=recv_sem.at[sweep, group, side],
                    device_id=target,
                    device_id_type=MESH,
                ),
                sends,
                gets,
            )
            for side, (a, b, target, sends, gets) in enumerate(ends)
        ]

    def begin(group):
        for copy, sends, _ in group:
            pl.when(sends)(copy.start)

    def landed(group):
        for copy, _, gets in group:
            pl.when(gets)(copy.wait_recv)

    def left(group):
        for copy, sends, _ in group:
            pl.when(sends)(copy.wait_send)

    first_vq = halo(0, VQ, start, v0, slice(0, 4), False, beside_first, slice(0, 4))
    first_eddy = halo(0, EDDY, start, v0, slice(4, 5), False, beside_first, slice(4, 5))
    first_base = halo(0, BASE, base, flow, slice(0, 3), False, beside_first, slice(5, 8))
    second_vq = halo(1, VQ, v1, v1, slice(0, 4), True, beside_second, slice(0, 4))
    second_eddy = halo(1, EDDY, v1, v1, slice(4, 5), True, beside_second, slice(4, 5))

    pl.semaphore_wait(barrier, n_plane + n_line)
    begin(first_vq)

    lane = lax.broadcasted_iota(I32, (cn, cz), 1)
    top, bottom = lane == cz - 1, lane == 0

    def loop(begin_at, end_at, body, together=1):
        def step_body(i, carry):
            for j in range(together):
                body(begin_at + i * together + j)
            return carry

        lax.fori_loop(0, (end_at - begin_at) // together, step_body, 0)

    for load in loads[:4]:
        load.wait()

    def prepare(e):
        w = 1.0 + visc[e]
        r1 = 1.0 / (6.0 * w + 1.0)
        half = 0.5 * r1
        wr = w * r1
        for k in range(3):
            hu = half * flow[k, e + 1, rows, :]
            above, below = wr + hu, wr - hu
            if k == 2:
                above, below = jnp.where(top, 0.0, above), jnp.where(bottom, 0.0, below)
            coef[2 * k, e] = above
            coef[2 * k + 1, e] = below
        coef[6, e] = half
        r2 = 1.0 / (6.0 * w + 2.0)
        rest[0, e] = r2
        rest[1, e] = w * r2

    loop(0, ce, prepare)
    begin(first_eddy)
    begin(first_base)

    entry_cell = cell[0]
    row_of = lax.shift_right_logical(entry_cell, cz.bit_length() - 1)
    level_of = lax.bitwise_and(entry_cell, cz - 1)
    level_hot = jnp.where(lax.broadcasted_iota(I32, (cz, slots), 0) == level_of, 1.0, 0.0).astype(BF16)
    levels[0:cz] = level_hot
    levels[cz : 2 * cz] = level_hot

    def gather(field, row_ids, comps):
        block_rows = field.shape[0] // comps
        both = jnp.concatenate(split(field), axis=1)
        found = jnp.dot(both, levels[...], preferred_element_type=F32)
        here = row_ids == row_of
        sums = []
        for c in range(comps):
            kept = jnp.where(here, found[c * block_rows : (c + 1) * block_rows], 0.0)
            sums.append(jnp.sum(kept.reshape(block_rows // 8, 8, slots), axis=0))
        return sums

    step = 4

    def upstream_block(p, acc):
        field = flow[0, pl.ds(p * step + 1, step), rows, :].reshape(step * cn, cz)
        row_ids = lax.broadcasted_iota(I32, (step * cn, slots), 0) + p * step * cn
        return acc + gather(field, row_ids, 1)[0]

    upstream = lax.fori_loop(0, ce // step, upstream_block, jnp.zeros((8, slots), F32))
    upstream = jnp.sum(upstream, axis=0, keepdims=True)
    live = lax.broadcasted_iota(I32, (1, slots), 1) < count[0, 0]
    factor = jnp.where(live, weight[0] * upstream * jnp.abs(upstream), 0.0)

    for load in loads[7:]:
        load.wait()
    turbine_of = turbine[0]
    owner_of = lax.shift_right_logical(turbine_of * 5462, 16)
    place_of = sector[0] * PITCH + turbine_of - owner_of * TURB_DEV
    block_of = 4 * lax.shift_right_logical(owner_of, 3) + lax.bitwise_and(owner_of, 3)
    part_of = 2 * block_of + lax.bitwise_and(lax.shift_right_logical(owner_of, 2), 1)
    places[...] = jnp.where(lax.broadcasted_iota(I32, places.shape, 0) == place_of, 1.0, 0.0).astype(BF16)
    row_iota = lax.broadcasted_iota(I32, blocks.shape, 0)
    part_iota = 2 * lax.shift_right_logical(row_iota, 4) + lax.bitwise_and(lax.shift_right_logical(row_iota, 2), 1)
    blocks[...] = jnp.where(part_iota == part_of, 1.0, 0.0).astype(BF16)

    def shifted(x):
        return pltpu.roll(x, cz - 1, 1), pltpu.roll(x, 1, 1)

    def relax_vq(e, old, new, offset, where_rows):
        def beside(c):
            x = old[c, e + 1, rows, :]
            return (
                x,
                old[c, e + 2, rows, :],
                old[c, e, rows, :],
                old[c, e + 1, pl.ds(PAD + 1, cn), :],
                old[c, e + 1, pl.ds(PAD - 1, cn), :],
                *shifted(x),
            )

        _, qe, qw, qn, qs, qu, qd = beside(3)
        qu, qd = jnp.where(top, 0.0, qu), jnp.where(bottom, 0.0, qd)
        grads = (qe - qw, qn - qs, qu - qd)
        sum_q = qe + qw + qn + qs + qu + qd
        half = coef[6, e]
        r1 = half + half
        diverge = None
        for c in range(3):
            _, *near = beside(c)
            total = r1 * src[c, e] - half * grads[c]
            for k in range(6):
                total = total + coef[k, e] * near[k]
            new[c, e + offset, where_rows, :] = total
            above, below = near[2 * c], near[2 * c + 1]
            if c == 2:
                above, below = jnp.where(top, 0.0, above), jnp.where(bottom, 0.0, below)
            slope = above - below
            diverge = slope if diverge is None else diverge + slope
        new[3, e + offset, where_rows, :] = (src[3, e] + sum_q - 0.5 * diverge) * (1.0 / 7.0)

    def around(ref, c, e):
        x = ref[c, e + 1, rows, :]
        up, down = shifted(x)
        up, down = jnp.where(top, 0.0, up), jnp.where(bottom, 0.0, down)
        total = ref[c, e + 2, rows, :] + ref[c, e, rows, :]
        total = total + ref[c, e + 1, pl.ds(PAD + 1, cn), :] + ref[c, e + 1, pl.ds(PAD - 1, cn), :]
        return total + up + down, x

    def relax_eddy(e, old, new, offset, where_rows, first):
        sum_m, _ = around(old, 4, e)
        total = rest[0, e] * src[4, e] + rest[1, e] * sum_m
        for c in range(3):
            if first:
                sum_u, u = around(flow, c, e)
                bend = (0.25 * rest[0, e]) * (sum_u - 6.0 * u)
                curve[c, e] = bend
            else:
                bend = curve[c, e]
            total = total + old[c, e + 1, rows, :] * bend
        new[4, e + offset, where_rows, :] = total

    def sides():
        return ((0, 0, 3, 1.0), (cn - 8, 8, 2, -1.0))

    def fix_vq(e, landing, new, offset, pad):
        for row, tile, k, sign in sides():
            near = [landing[c, e, tile : tile + 8, :] for c in range(4)]
            here = slice(row, row + 8)
            for c in range(3):
                add = coef[k, e, here, :] * near[c]
                if c == 1:
                    add = add + (sign * coef[6, e, here, :]) * near[3]
                new[c, e + offset, pad + row : pad + row + 8, :] += add
            new[3, e + offset, pad + row : pad + row + 8, :] += (near[3] + (0.5 * sign) * near[1]) * (1.0 / 7.0)

    def fix_eddy(e, landing, old, new, offset, pad, first):
        for row, tile, _, _ in sides():
            here = slice(row, row + 8)
            add = rest[1, e, here, :] * landing[4, e, tile : tile + 8, :]
            if first:
                quarter = 0.25 * rest[0, e, here, :]
                for c in range(3):
                    bend = quarter * landing[5 + c, e, tile : tile + 8, :]
                    curve[c, e, here, :] += bend
                    add = add + old[c, e + 1, PAD + row : PAD + row + 8, :] * bend
            new[4, e + offset, pad + row : pad + row + 8, :] += add

    for load in loads[4:7]:
        load.wait()
    vq_one = lambda e: relax_vq(e, v0, v1, 1, rows)
    eddy_one = lambda e: relax_eddy(e, v0, v1, 1, rows, True)
    loop(1, ce - 1, vq_one)
    loop(1, ce - 1, eddy_one)
    landed(first_vq)
    vq_one(0)
    vq_one(ce - 1)
    loop(0, ce, lambda e: fix_vq(e, beside_first, v1, 1, PAD), 4)
    begin(second_vq)
    vq_two = lambda e: relax_vq(e, v1, final, 0, slice(None))
    loop(1, ce - 1, vq_two)
    half_inside = (ce - 2) // 2

    def inner_ids(count_rows, first_row):
        ids = lax.broadcasted_iota(I32, (count_rows, slots), 0)
        in_plane_row = lax.rem(ids, cn)
        return jnp.where((in_plane_row == 0) | (in_plane_row == cn - 1), -1, ids + first_row)

    def gather_inside(c):
        acc = jnp.zeros((8, slots), F32)
        for part in range(2):
            p = 1 + part * half_inside
            field = final[c, p : p + half_inside].reshape(half_inside * cn, cz)
            acc = acc + gather(field, inner_ids(half_inside * cn, p * cn), 1)[0]
        found_acc[c] = acc

    loop(0, 2, gather_inside)
    landed(first_eddy)
    landed(first_base)
    fix_eddy_one = lambda e: fix_eddy(e, beside_first, v0, v1, 1, PAD, True)
    for e in (0, ce - 1):
        eddy_one(e)
        fix_eddy_one(e)
    begin(second_eddy[:2])
    loop(1, ce - 1, fix_eddy_one, 2)
    begin(second_eddy[2:])

    eddy_two = lambda e: relax_eddy(e, v1, final, 0, slice(None), False)
    loop(1, ce - 1, eddy_two)
    gather_inside(2)
    gather_inside(4)
    landed(second_vq)
    vq_two(0)
    vq_two(ce - 1)
    loop(0, ce, lambda e: fix_vq(e, beside_second, final, 0, 0), 4)
    plane_iota = lax.broadcasted_iota(I32, (ce, slots), 0) * cn

    def gather_edges(comps):
        edge_ids = jnp.concatenate(
            [inner_ids(cn, 0), inner_ids(cn, (ce - 1) * cn), plane_iota, plane_iota + cn - 1], axis=0
        )
        edge_fields = []
        for c in comps:
            edge_fields += [final[c, plane] for plane in (0, ce - 1)]
            edge_fields += [final[c, :, row, :] for row in (0, cn - 1)]
        return gather(jnp.concatenate(edge_fields, axis=0), edge_ids, len(comps))

    edge_sums = gather_edges((0, 1, 2))
    landed(second_eddy)
    eddy_two(0)
    eddy_two(ce - 1)
    loop(0, ce, lambda e: fix_eddy(e, beside_second, v1, final, 0, 0, False), 4)

    edge_sums += gather_edges((4,))
    values = [
        jnp.sum(found_acc[c] + edge, axis=0, keepdims=True) * factor for c, edge in zip((0, 1, 2, 4), edge_sums)
    ]
    terms = jnp.concatenate(values + values, axis=0)
    both = jnp.concatenate(split(terms), axis=0)
    spread = blocks[...] * jnp.concatenate([both] * n_plane, axis=0)
    contract = (((1,), (1,)), ((), ()))
    summed = lax.dot_general(spread, places[...], contract, preferred_element_type=F32)
    parts[...] = jnp.sum(summed.reshape(n_plane, 2, 8, SECT * PITCH), axis=1)

    part_copies, total_copies = [], []
    for k in range(1, n_plane):
        to, target = plane_peer(k)
        part_copies.append(
            pltpu.make_async_remote_copy(
                src_ref=parts.at[to],
                dst_ref=gathered.at[in_plane],
                send_sem=part_send.at[k],
                recv_sem=part_recv.at[k],
                device_id=target,
                device_id_type=MESH,
            )
        )
    for k in range(1, n_line):
        to, target = line_peer(k)
        total_copies.append(
            pltpu.make_async_remote_copy(
                src_ref=middle.at[to % 2],
                dst_ref=totals.at[in_line],
                send_sem=total_send.at[k],
                recv_sem=total_recv.at[k],
                device_id=target,
                device_id_type=MESH,
            )
        )
    for copy in part_copies:
        copy.start()
    gathered[in_plane] = parts[in_plane]
    for group in (first_vq, first_base, first_eddy, second_vq, second_eddy):
        left(group)
    for copy in part_copies:
        copy.wait_recv()
    in_middle = jnp.sum(gathered[...], axis=0)
    middle[0] = in_middle[0:4]
    middle[1] = in_middle[4:8]
    for copy in total_copies:
        copy.start()
    totals[in_line] = middle[low_z]
    for copy in part_copies:
        copy.wait_send()
    for copy in total_copies:
        copy.wait_recv()
    whole = jnp.sum(totals[...], axis=0)
    for s in range(SECT):
        cut = whole[:, s * PITCH : s * PITCH + TURB_DEV]
        for c in range(4):
            grad[c, s : s + 1, :] = cut[c : c + 1]

    for copy in total_copies:
        copy.wait_send()


def store(fields, sums, fields_out, sums_out, sem):
    copies = [pltpu.make_async_copy(sums, sums_out, sem.at[0])]
    copies += [pltpu.make_async_copy(fields.at[c], fields_out.at[c], sem.at[c + 1]) for c in range(fields.shape[0])]
    for copy in copies:
        copy.start()
    for copy in copies:
        copy.wait()


def shards(n_east, n_north, *arrays):
    start, source, base, eddy, count, cell = arrays[:6]
    _, ce, cn, cz = start.shape
    slots = cell.shape[-1]
    padded = (ce + 2, cn + 2 * PAD, cz)
    n_plane, n_line = n_north // 2, n_east * 2
    hbm, vmem = pl.BlockSpec(memory_space=pltpu.HBM), pl.BlockSpec(memory_space=pltpu.VMEM)
    in_vmem = (
        pl.pallas_call(
            functools.partial(kernel, n_east, n_north),
            out_shape=(pltpu.VMEM(start.shape, F32), pltpu.VMEM((4, SECT, TURB_DEV), F32)),
            in_specs=[hbm] * 4 + [pl.BlockSpec(memory_space=pltpu.SMEM)] + [hbm] * 4,
            out_specs=(vmem, vmem),
            scratch_shapes=[
                pltpu.VMEM((5, *padded), F32),
                pltpu.VMEM((5, *padded), F32),
                pltpu.VMEM((3, *padded), F32),
                pltpu.VMEM((ce, cn, cz), F32),
                pltpu.VMEM((5, ce, cn, cz), F32),
                pltpu.VMEM((7, ce, cn, cz), F32),
                pltpu.VMEM((2, ce, cn, cz), F32),
                pltpu.VMEM((3, ce, cn, cz), F32),
                pltpu.VMEM((2 * cz, slots), BF16),
                pltpu.VMEM((5, 8, slots), F32),
                pltpu.VMEM((SECT * PITCH, slots), BF16),
                pltpu.VMEM((n_plane * 16, slots), BF16),
                pltpu.VMEM((8, ce, 16, cz), F32),
                pltpu.VMEM((5, ce, 16, cz), F32),
                pltpu.VMEM((1, 1, slots), I32),
                pltpu.VMEM((1, 1, slots), I32),
                pltpu.VMEM((1, 1, slots), I32),
                pltpu.VMEM((1, 1, slots), F32),
                pltpu.VMEM((n_plane, 8, SECT * PITCH), F32),
                pltpu.VMEM((n_plane, 8, SECT * PITCH), F32),
                pltpu.VMEM((2, 4, SECT * PITCH), F32),
                pltpu.VMEM((n_line, 4, SECT * PITCH), F32),
                pltpu.SemaphoreType.DMA((9,)),
                pltpu.SemaphoreType.DMA((2, 3, 4)),
                pltpu.SemaphoreType.DMA((2, 3, 4)),
                pltpu.SemaphoreType.DMA((n_plane,)),
                pltpu.SemaphoreType.DMA((n_plane,)),
                pltpu.SemaphoreType.DMA((n_line,)),
                pltpu.SemaphoreType.DMA((n_line,)),
            ],
            compiler_params=pltpu.CompilerParams(
                collective_id=0, has_side_effects=True, vmem_limit_bytes=40 * 1024 * 1024
            ),
        )(*(pltpu.with_memory_space_constraint(x, pltpu.HBM) if x.dtype == F32 or x.ndim > 2 else x for x in arrays))
    )
    parts = start.shape[0]
    return tuple(
        pl.pallas_call(
            store,
            out_shape=tuple(jax.ShapeDtypeStruct(x.shape, x.dtype) for x in in_vmem),
            in_specs=[vmem] * 2,
            out_specs=(hbm, hbm),
            scratch_shapes=[pltpu.SemaphoreType.DMA((parts + 1,))],
            compiler_params=pltpu.CompilerParams(vmem_limit_bytes=8 * 1024 * 1024),
        )(*(pltpu.with_memory_space_constraint(x, pltpu.VMEM) for x in in_vmem))
    )


def solution(mesh):
    fields, scalars = P(None, "east", "north", None), P("east", "north", None)
    return jax.shard_map(
        functools.partial(shards, mesh.shape["east"], mesh.shape["north"]),
        mesh=mesh,
        in_specs=(fields, fields, fields, scalars, P("east", "north"), scalars, scalars, scalars, scalars),
        out_specs=(fields, P(None, None, "north")),
        check_vma=False,
    )
```
